512 devices in a mesh: dp: 16 (over z, core), cent: 32 (over y, x).
Axes of the slice: x: 4, y: 8, z: 8, core: 2. Of those that a mesh axis runs over, the one named last changes fastest.
Arguments:
- embeddings: bfloat16 [12288, 1024], P(('dp', 'cent')), as said below
- outcomes: int32 [12288], P(('dp', 'cent')), may hold values 0 or 1
- seed_index: int32 [32768], P('cent'), may hold values from 0 to 12287
Outputs:
- centroids: bfloat16 [32768, 1024], P(('cent', 'dp'))
- step_scores: float32 [12288], P(('dp', 'cent'))
The draws below stay inside these ranges and needn't reach their ends.
Inputs may be any that keep to these rules, and one draw needn't show every extreme that they name: `embeddings`: entries are bounded in magnitude by 44 / sqrt(1024).
All inputs are finite; a program needn't handle non-finite values. No bound on the sum of `outcomes` on one device may be relied on, other than what follows from the above.
Results may differ from the reference program's by a relative error of at most 0.01.
Values may be sent and summed in bfloat16 or wider, within the bound.
A program may use at most 64 MiB of HBM per device.

```python
import jax
import jax.numpy as jnp
from jax import lax

D = 1024
R_DEV = 24
ITERS = 2
N = 12288
K = 32768
N_CENT = 32


def draw_embeddings(key, part):
    first_key = jax.random.fold_in(key, 11)
    second_key = jax.random.fold_in(key, 12)
    base = jnp.clip(jax.random.normal(first_key, (N, D), jnp.float32), -5.0, 5.0) * D ** (-0.5)
    scales = jnp.exp(jax.random.uniform(second_key, (N, 1), jnp.float32, -0.35, 0.35))
    result = base * scales
    return result.astype(jnp.bfloat16)


def place_ends(entries, rng, least, high):
    dims = entries.shape
    place = [jax.random.randint(jax.random.fold_in(rng, axis), (), 0, dims[axis]) for axis in range(len(dims))]
    entries = entries.at[tuple(place)].set(least)
    longest = dims.index(max(dims))
    place[longest] = (place[longest] + 1) % dims[longest]
    return entries.at[tuple(place)].set(high)


def setup_inputs(seed: int = 0) -> dict:
    streams_of = jax.random.split(jax.random.key(seed), 4)
    return {
        "embeddings": draw_embeddings(jax.random.fold_in(streams_of[3], 71), 0),
        "outcomes": place_ends((jax.random.randint(streams_of[1], (N,), 0, 2) < 1).astype(jnp.int32), jax.random.fold_in(streams_of[1], 1), 0, 1),
        "seed_index": place_ends(jax.random.randint(streams_of[2], (K,), 0, N), jax.random.fold_in(streams_of[2], 1), 0, N - 1).astype(jnp.int32),
    }


INVERSE_TEMP = 8.0
PSEUDO_COUNT = 1.0


def soft_weights(row_block, centroid_set, sq_norms):
    products = lax.dot_general(row_block, centroid_set, (((1,), (1,)), ((), ())), preferred_element_type=jnp.float32)
    logits = INVERSE_TEMP * (products - 0.5 * sq_norms[None, :])
    row_max = jnp.max(logits, axis=1, keepdims=True)
    exponent = jnp.exp(logits - row_max)
    return exponent / jnp.sum(exponent, axis=1, keepdims=True)


def reference(embeddings, outcomes, seed_index):
    group_rows = R_DEV * N_CENT
    blocks = embeddings.shape[0] // group_rows
    tok_blocks = embeddings.reshape(blocks, group_rows, D)
    lab_blocks = outcomes.astype(jnp.bfloat16).reshape(blocks, group_rows)
    centroid_set = jnp.take(embeddings, seed_index.astype(jnp.int32), axis=0)
    previous = centroid_set
    sq_norms = jnp.zeros((K,), jnp.float32)
    masses = jnp.zeros((K,), jnp.float32)
    successes = jnp.zeros((K,), jnp.float32)
    for iteration in range(ITERS):
        sq_norms = jnp.sum(jnp.square(centroid_set.astype(jnp.float32)), axis=1)
        current = centroid_set

        def accumulate(state_sums, item_pair):
            numerator, mass_sum, win_sum = state_sums
            row_block, labels = item_pair
            rounded = soft_weights(row_block, current, sq_norms).astype(jnp.bfloat16)
            partial_value = lax.dot_general(rounded, row_block, (((0,), (0,)), ((), ())), preferred_element_type=jnp.float32)
            partial_value = lax.optimization_barrier(partial_value.astype(jnp.bfloat16)).astype(jnp.float32)
            mass_sum = mass_sum + jnp.sum(rounded, axis=0, dtype=jnp.float32)
            win_sum = win_sum + jnp.dot(labels, rounded, preferred_element_type=jnp.float32)
            return (numerator + partial_value, mass_sum, win_sum), None

        zeros_init = (jnp.zeros((K, D), jnp.float32), jnp.zeros((K,), jnp.float32), jnp.zeros((K,), jnp.float32))
        (numerator, masses, successes), _ = lax.scan(accumulate, zeros_init, (tok_blocks, lab_blocks))
        previous = current
        centroid_set = ((numerator + PSEUDO_COUNT * current.astype(jnp.float32)) / (masses + PSEUDO_COUNT)[:, None]).astype(jnp.bfloat16)
    success_rate = (successes + 0.5 * PSEUDO_COUNT) / (masses + PSEUDO_COUNT)

    def score_block(row_block):
        weights = soft_weights(row_block, previous, sq_norms)
        return jnp.dot(weights, success_rate, precision=lax.Precision.HIGHEST)

    step_scores = lax.map(score_block, tok_blocks).reshape(-1)
    return centroid_set, step_scores
```

```python
import functools

import jax
import jax.numpy as jnp
from jax import lax
from jax.experimental import pallas as pl
from jax.experimental.pallas import tpu as pltpu
from jax.sharding import PartitionSpec as P

INVERSE_TEMP = 8.0
PSEUDO_COUNT = 1.0
ABSENT = -1e30
MESH = pl.DeviceIdType.MESH
F32 = jnp.float32
BF16 = jnp.bfloat16


class Sizes:
    def __init__(self, z, y, x, rows, features, seeds):
        self.z, self.y, self.x = z, y, x
        self.rows = rows
        self.chip = 2 * rows
        self.features = features
        self.half = features // 2
        self.slab = features // z
        self.local = (z // 2) * self.chip
        self.group = y * x * self.chip
        self.blocks = 4 if y >= 4 else 1
        self.width = self.group // self.blocks
        self.seeds = seeds
        self.outs = seeds // (2 * z)
        self.lanes = -(-self.local // 128) * 128


def scratch_of(s):
    dma = pltpu.SemaphoreType.DMA
    v = pltpu.VMEM
    return dict(
        mine=v((32, s.features), BF16),
        theirs=v((32, s.features), BF16),
        block=v((s.chip, s.features), BF16),
        rows=v((s.y, s.x, s.chip, s.features), BF16),
        cents=v((2, s.local, s.features), BF16),
        lab_x=v((2, s.x, 1, s.width), F32),
        lab_s=v((1, s.width), F32),
        lab_y=v((s.y, 1, s.width), F32),
        cnt_s=v((s.x, s.y, s.lanes), F32),
        cnt_x=v((s.x, s.y, s.lanes), F32),
        cnt_t=v((s.y, 1, s.lanes), F32),
        cnt_y=v((s.y, 1, s.lanes), F32),
        logits=v((s.blocks, s.local, s.width), F32),
        probs=v((s.blocks, s.local, s.width), BF16),
        st_s=v((3, s.blocks, 1, s.width), F32),
        st_x=v((3, 2, s.x, s.blocks, 1, s.width), F32),
        st_t=v((3, s.blocks, 1, s.width), F32),
        st_y=v((3, s.y, s.blocks, 1, s.width), F32),
        mw_s=v((2, 8, s.lanes), F32),
        mw_r=v((2, s.z, 8, s.lanes), F32),
        num_s=v((2, s.z, s.local, s.slab), BF16),
        num_r=v((2, s.z, s.local, s.slab), BF16),
        table=v((2, s.y, s.x, s.local, s.slab), BF16),
        wide=v((2 * s.y * s.x * s.local, s.slab), F32),
        picked=v((s.outs, s.slab), F32),
        out_s=v((s.z, s.outs, s.slab), BF16),
        out_r=v((s.z, s.outs, s.slab), BF16),
        core_sem=dma((2, 3)),
        a1_sem=dma((2, 2, s.x)),
        a2_sem=dma((2, 2, s.y)),
        b1_sem=dma((2, 2, s.y)),
        b2_sem=dma((2, 2, s.x)),
        cent_sem=dma((2, s.z)),
        lab_sem=dma((2, 2 * s.x)),
        laby_sem=dma((2, s.y)),
        cnt_sem=dma((2, s.x)),
        cnty_sem=dma((2, s.y)),
        stx_sem=dma((3, 2, 2 * s.x)),
        sty_sem=dma((3, 2, s.y)),
        mw_sem=dma((2, 2, s.z)),
        num_sem=dma((2, 2, s.z)),
        new_sem=dma((2, s.z)),
        out_sem=dma((2, s.z)),
    )


def kernel(s, names, emb, lab, qr, pos, out_c, out_v, *scratch):
    ref = dict(zip(names, scratch))
    dp, cent = lax.axis_index("dp"), lax.axis_index("cent")
    z, core = dp // 2, dp % 2
    y, x = cent // s.x, cent % s.x

    def device(z_, core_, y_, x_):
        return (z_ * 2 + core_, y_ * s.x + x_)

    to_z = lambda p: device(p, core, y, x)
    to_y = lambda p: device(z, core, p, x)
    to_x = lambda p: device(z, core, y, p)
    to_cx = lambda p: device(z, p // s.x, y, p % s.x)
    partner = device(z, 1 - core, y, x)
    cx = core * s.x + x

    def each(n, me, do):
        def step(i, carry):
            do(lax.rem(me + i, n))
            return carry

        lax.fori_loop(1, n, step, 0)

    def copy(src, dst, sems, out_index, in_index, to):
        return pltpu.make_async_remote_copy(
            src_ref=src,
            dst_ref=dst,
            send_sem=sems.at[0, out_index],
            recv_sem=sems.at[1, in_index],
            device_id=to,
            device_id_type=MESH,
        )

    pending = []

    class Exchange:
        def __init__(self, n, me, to, sems, src, dst):
            self.n, self.me, self.to, self.sems, self.src, self.dst = n, me, to, sems, src, dst

        def start(self):
            each(self.n, self.me, lambda p: copy(
                self.src(p), self.dst(self.me), self.sems, p, self.me, self.to(p)).start())
            pending.append(self)

        def arrived(self):
            each(self.n, self.me, lambda p: copy(
                self.src(p), self.dst(p), self.sems, p, p, self.to(p)).wait_recv())

        def sent(self):
            each(self.n, self.me, lambda p: copy(
                self.src(p), self.dst(self.me), self.sems, p, self.me, self.to(p)).wait_send())

    barrier = pltpu.get_barrier_semaphore()

    def greet(to):
        return lambda p: pl.semaphore_signal(barrier, inc=1, device_id=to(p), device_id_type=MESH)

    each(2 * s.x, cx, greet(to_cx))
    each(s.y, y, greet(to_y))
    each(s.z, z, greet(to_z))
    pl.semaphore_wait(barrier, 2 * s.x - 1 + s.y - 1 + s.z - 1)

    mine, theirs = ref["mine"], ref["theirs"]
    mine[...] = jnp.concatenate(
        [emb[...].astype(F32), jnp.zeros((32 - s.rows, s.features), F32)], axis=0
    ).astype(BF16)
    swap = pltpu.make_async_remote_copy(
        src_ref=mine, dst_ref=theirs, send_sem=ref["core_sem"].at[0, 0],
        recv_sem=ref["core_sem"].at[1, 0], device_id=partner, device_id_type=MESH,
    )
    swap.start()

    lab_x = ref["lab_x"]
    lab_x[core, x] = lab[...]
    lab_ex = Exchange(2 * s.x, cx, to_cx, ref["lab_sem"],
                      lambda p: lab_x.at[core, x], lambda p: lab_x.at[p // s.x, p % s.x])
    lab_ex.start()

    cnt_s, cnt_x = ref["cnt_s"], ref["cnt_x"]
    places = lax.broadcasted_iota(jnp.int32, (s.lanes, s.seeds), 0)
    hot_r = jnp.where(places == qr[1:2, :], 1.0, 0.0).astype(BF16)
    for xx in range(s.x):
        owner = lax.broadcasted_iota(jnp.int32, (s.y, s.seeds), 0) * s.x + (xx + core * s.x * s.y)
        hot_q = jnp.where(owner == qr[0:1, :], 1.0, 0.0).astype(BF16)
        cnt_s[xx] = lax.dot_general(hot_q, hot_r, (((1,), (1,)), ((), ())), preferred_element_type=F32)
    cnt_ex = Exchange(s.x, x, to_x, ref["cnt_sem"], lambda p: cnt_s.at[p], lambda p: cnt_x.at[p])
    cnt_ex.start()

    swap.wait_recv()
    own = mine[...].astype(F32)[: s.rows]
    other = theirs[...].astype(F32)[: s.rows]
    rows, block = ref["rows"], ref["block"]
    first = jnp.where(core == 0, own, other)
    second = jnp.where(core == 0, other, own)
    block[...] = jnp.concatenate([first, second], axis=0).astype(BF16)

    def plane(t, at, tall, low, forward_from, forward_to):
        top, rest = pl.ds(0, low), pl.ds(low, tall - low)
        a1 = Exchange(s.x, x, to_x, ref["a1_sem"].at[t], lambda p: at(y, x, top), lambda p: at(y, p, top))
        b1 = Exchange(s.y, y, to_y, ref["b1_sem"].at[t], lambda p: at(y, x, rest), lambda p: at(p, x, rest))
        every = slice(None)
        a2 = Exchange(s.y, y, to_y, ref["a2_sem"].at[t], lambda p: at(y, every, top), lambda p: at(p, every, top))
        b2 = Exchange(s.x, x, to_x, ref["b2_sem"].at[t], lambda p: at(every, x, rest), lambda p: at(every, p, rest))
        a1.start()
        b1.start()
        yield
        a1.arrived()
        a2.start()
        b1.arrived()
        b2.start()
        yield
        a2.arrived()
        b2.arrived()
        share = pltpu.make_async_remote_copy(
            src_ref=forward_from, dst_ref=forward_from, send_sem=ref["core_sem"].at[0, 1 + t],
            recv_sem=ref["core_sem"].at[1, 1 + t], device_id=partner, device_id_type=MESH,
        )
        share.start()
        yield
        pltpu.make_async_remote_copy(
            src_ref=forward_from, dst_ref=forward_to, send_sem=ref["core_sem"].at[0, 1 + t],
            recv_sem=ref["core_sem"].at[1, 1 + t], device_id=partner, device_id_type=MESH,
        ).wait_recv()
        share.wait_send()

    def lanes_of(c):
        return pl.ds(pl.multiple_of(c * s.half, 128), s.half)

    rows[y, x, :, lanes_of(core)] = block[:, lanes_of(core)]
    gather = plane(
        0,
        lambda yy, xx, part: rows.at[yy, xx, part, lanes_of(core)],
        s.chip,
        16,
        rows.at[:, :, :, lanes_of(core)],
        rows.at[:, :, :, lanes_of(1 - core)],
    )
    next(gather)

    cents = ref["cents"]
    zh = s.z // 2

    def cent_copy(src_z, to):
        place = pl.ds(pl.multiple_of((src_z % zh) * s.chip, 16), s.chip)
        return copy(block, cents.at[0, place, :], ref["cent_sem"], to, src_z, to_z(to))

    @pl.when(z // zh == core)
    def _():
        each(s.z, z, lambda p: cent_copy(z, p).start())
        cents[0, pl.ds(pl.multiple_of((z % zh) * s.chip, 16), s.chip), :] = block[...]

    cnt_ex.arrived()
    cnt_x[x] = cnt_s[x]
    total = cnt_x[0]
    for xx in range(1, s.x):
        total = total + cnt_x[xx]
    cnt_t, cnt_y = ref["cnt_t"], ref["cnt_y"]
    for yy in range(s.y):
        cnt_t[yy] = total[yy : yy + 1]
    cnty_ex = Exchange(s.y, y, to_y, ref["cnty_sem"], lambda p: cnt_t.at[p], lambda p: cnt_y.at[p])
    cnty_ex.start()
    lab_ex.arrived()
    lab_s, lab_y = ref["lab_s"], ref["lab_y"]
    line = lab_x[0, 0]
    for i in range(1, 2 * s.x):
        line = line + lab_x[i // s.x, i % s.x]
    lab_y[y] = line
    laby_ex = Exchange(s.y, y, to_y, ref["laby_sem"], lambda p: lab_y.at[y], lambda p: lab_y.at[p])
    laby_ex.start()

    next(gather)

    def to_column(row):
        eye = lax.broadcasted_iota(jnp.int32, (s.local, s.lanes), 0) == lax.broadcasted_iota(
            jnp.int32, (s.local, s.lanes), 1
        )
        return jnp.sum(jnp.where(eye, row, 0.0), axis=1, keepdims=True)

    cnty_ex.arrived()
    cnt_y[y] = cnt_t[y]
    line = cnt_y[0]
    for yy in range(1, s.y):
        line = line + cnt_y[yy]
    weight = to_column(line)
    laby_ex.arrived()

    @pl.when(z // zh == core)
    def _():
        each(s.z, z, lambda p: cent_copy(z, p).wait_send())

    def cents_in(i, carry):
        src_z = core * zh + i

        @pl.when(src_z != z)
        def _():
            place = pl.ds(pl.multiple_of(i * s.chip, 16), s.chip)
            copy(block, cents.at[0, place, :], ref["cent_sem"], src_z, src_z, to_z(src_z)).wait_recv()

        return carry

    lax.fori_loop(0, zh, cents_in, 0)
    next(gather)
    for _ in gather:
        pass

    def rows_of(b, lanes):
        per = s.y // s.blocks
        return rows[pl.ds(b * per, per), :, :, lanes].reshape(s.width, -1)

    logits, probs = ref["logits"], ref["probs"]
    everything = slice(None)

    def blocks(do):
        def step(b, carry):
            do(b)
            return carry

        lax.fori_loop(0, s.blocks, step, 0)

    def lse_of(parts):
        top = functools.reduce(jnp.maximum, parts)
        return top + jnp.log(sum(jnp.exp(part - top) for part in parts))

    def total_of(parts):
        return sum(parts)

    def all_reduce(t, combine):
        st_s, st_x, st_t, st_y = (ref[name].at[t] for name in ("st_s", "st_x", "st_t", "st_y"))
        near = Exchange(2 * s.x, cx, to_cx, ref["stx_sem"].at[t], lambda p: st_s, lambda p: st_x.at[p // s.x, p % s.x])
        far = Exchange(s.y, y, to_y, ref["sty_sem"].at[t], lambda p: st_t, lambda p: st_y.at[p])
        near.start()
        yield
        near.arrived()
        st_x[core, x] = st_s[...]
        st_t[...] = combine([st_x[i // s.x, i % s.x] for i in range(2 * s.x)])
        far.start()
        yield
        far.arrived()
        st_y[y] = st_t[...]
        st_s_final[t][...] = combine([st_y[i] for i in range(s.y)])

    st_s_final = [ref["st_x"].at[t, 0, 0] for t in range(3)]

    for t in range(2):
        held = cents.at[t]
        wide = held[...].astype(F32)
        norm = jnp.sum(wide * wide, axis=1, keepdims=True)
        bias = jnp.where(weight > 0.0, (-0.5 * INVERSE_TEMP) * norm, ABSENT)
        st_s = ref["st_s"].at[t]

        def scores_of(b):
            product = lax.dot_general(
                held[...], rows_of(b, everything), (((1,), (1,)), ((), ())), preferred_element_type=F32
            )
            value = INVERSE_TEMP * product + bias
            value = jnp.where(weight > 0.0, value, ABSENT)
            logits[b] = value
            top = jnp.max(value, axis=0, keepdims=True)
            mass = jnp.sum(weight * jnp.exp(value - top), axis=0, keepdims=True)
            st_s[b] = jnp.maximum(top + jnp.log(mass), ABSENT)

        blocks(scores_of)
        for _ in all_reduce(t, lse_of):
            pass
        norm_of = st_s_final[t]
        mw_s, mw_r = ref["mw_s"].at[t], ref["mw_r"].at[t]
        mw_s[...] = jnp.zeros_like(mw_s)

        def shares_of(b):
            value = jnp.exp(logits[b] - norm_of[b])
            if t == 1:
                logits[b] = value
            rounded = value.astype(BF16)
            probs[b] = rounded
            per = s.y // s.blocks
            label = lab_y[b * per]
            for i in range(1, per):
                label = label + lab_y[b * per + i]
            line = lax.broadcasted_iota(jnp.int32, (8, s.width), 0)
            left = jnp.where(line == 0, 1.0, jnp.where(line == 1, label, 0.0)).astype(BF16)
            both = lax.dot_general(left, rounded, (((1,), (1,)), ((), ())), preferred_element_type=F32)
            mw_s[:, : s.local] += both

        blocks(shares_of)
        mw_ex = Exchange(s.z, z, to_z, ref["mw_sem"].at[t], lambda p: mw_s, lambda p: mw_r.at[p])
        mw_ex.start()

        num_s, num_r = ref["num_s"].at[t], ref["num_r"].at[t]
        num_ex = Exchange(s.z, z, to_z, ref["num_sem"].at[t], lambda p: num_s.at[p], lambda p: num_r.at[p])
        pairs = s.z // 2

        def numer_of(i, carry):
            pair = lax.rem(z // 2 + 1 + i, pairs)
            lanes = pl.ds(pl.multiple_of(pair * 2 * s.slab, 128), 2 * s.slab)
            acc = jnp.zeros((s.local, 2 * s.slab), F32)
            for b in range(s.blocks):
                acc = acc + jnp.dot(probs[b], rows_of(b, lanes), preferred_element_type=F32)
            for side in range(2):
                p = pair * 2 + side
                num_s[p] = acc[:, side * s.slab : (side + 1) * s.slab].astype(BF16)

                @pl.when(p != z)
                def _():
                    copy(num_s.at[p], num_r.at[z], ref["num_sem"].at[t], p, z, to_z(p)).start()

            return carry

        lax.fori_loop(0, pairs, numer_of, 0)
        pending.append(num_ex)
        mw_ex.arrived()
        mw_r[z] = mw_s[...]
        both = mw_r[0]
        for i in range(1, s.z):
            both = both + mw_r[i]
        mass = to_column(both[0:1])
        if t == 1:
            wins = to_column(both[1:2])
            rate = weight * ((wins + 0.5 * PSEUDO_COUNT) / (mass + PSEUDO_COUNT))
            sc = ref["st_s"].at[2]

            def step_scores(b):
                sc[b] = jnp.sum(logits[b] * rate, axis=0, keepdims=True)

            blocks(step_scores)
            reduce_scores = all_reduce(2, total_of)
            next(reduce_scores)
        num_ex.arrived()
        num_r[z] = num_s[z]
        mylanes = pl.ds(pl.multiple_of(z * s.slab, 128), s.slab)
        acc = num_r[0].astype(F32)
        for i in range(1, s.z):
            acc = acc + num_r[i].astype(F32)
        acc = acc + PSEUDO_COUNT * held[:, mylanes].astype(F32)
        fresh = (acc / (mass + PSEUDO_COUNT)).astype(BF16)
        if t == 0:
            cents[1, :, mylanes] = fresh

            def slab_at(p):
                return cents.at[1, :, pl.ds(pl.multiple_of(p * s.slab, 128), s.slab)]

            new_ex = Exchange(s.z, z, to_z, ref["new_sem"], lambda p: slab_at(z), slab_at)
            new_ex.start()
            new_ex.arrived()

    table, wide = ref["table"], ref["wide"]
    table[core, y, x] = fresh
    gather = plane(
        1,
        lambda yy, xx, part: table.at[core, yy, xx, part, :],
        s.local,
        s.local // 3,
        table.at[core],
        table.at[1 - core],
    )
    next(gather)
    next(reduce_scores)
    next(gather)
    for _ in reduce_scores:
        pass
    final = st_s_final[2]
    offset = cent * s.chip + core * s.rows
    n_out = 32
    column = jnp.zeros((n_out, 1), F32)
    for b in range(s.blocks):
        here = lax.broadcasted_iota(jnp.int32, (n_out, s.width), 1) + b * s.width
        wanted = lax.broadcasted_iota(jnp.int32, (n_out, s.width), 0) + offset
        column = column + jnp.sum(jnp.where(here == wanted, final[b], 0.0), axis=1, keepdims=True)
    eye = lax.broadcasted_iota(jnp.int32, (n_out, 128), 0) == lax.broadcasted_iota(jnp.int32, (n_out, 128), 1)
    out_v[...] = jnp.sum(jnp.where(eye, column, 0.0), axis=0, keepdims=True)

    next(gather)
    for _ in gather:
        pass

    def widen(i, carry):
        a, yy = i // s.y, i % s.y
        size = s.x * s.local
        wide[pl.ds(pl.multiple_of(i * size, 16), size), :] = (
            table[a, yy].reshape(size, s.slab).astype(F32)
        )
        return carry

    lax.fori_loop(0, 2 * s.y, widen, 0)
    picked, out_s, out_r = ref["picked"], ref["out_s"], ref["out_r"]
    out_ex = Exchange(s.z, z, to_z, ref["out_sem"], lambda p: out_s.at[p], lambda p: out_r.at[p])

    def pick(i, carry):
        p = lax.rem(z + 1 + i, s.z)
        base = (2 * p + core) * s.outs

        def eight(j, carry):
            for k in range(8):
                n = j * 8 + k
                picked[pl.ds(n, 1), :] = wide[pl.ds(pos[base + n], 1), :]
            return carry

        lax.fori_loop(0, s.outs // 8, eight, 0)
        out_s[p] = picked[...].astype(BF16)

        @pl.when(p != z)
        def _():
            copy(out_s.at[p], out_r.at[z], ref["out_sem"], p, z, to_z(p)).start()

        return carry

    lax.fori_loop(0, s.z, pick, 0)
    pending.append(out_ex)
    out_ex.arrived()
    out_r[z] = out_s[z]
    for i in range(s.z):
        out_c[:, i * s.slab : (i + 1) * s.slab] = out_r[i]
    swap.wait_send()
    for exchange in pending:
        exchange.sent()


def per_device(s, embeddings, outcomes, seed_index):
    core = lax.axis_index("dp") % 2
    cent = lax.axis_index("cent")
    plane = s.rows * s.x * s.y
    dp, rest = seed_index // plane, seed_index % plane
    zs, side = dp // 2, dp % 2
    zh = s.z // 2
    q = (zs // zh) * (s.x * s.y) + rest // s.rows
    r = (zs % zh) * s.chip + side * s.rows + rest % s.rows
    qr = jnp.stack([q, r])
    pos = q * s.local + r
    offset = (cent * s.chip) % s.width + core * s.rows
    spot = lax.broadcasted_iota(jnp.int32, (s.rows, s.width), 1) - lax.broadcasted_iota(
        jnp.int32, (s.rows, s.width), 0
    )
    lab = jnp.sum(
        jnp.where(spot == offset, outcomes.astype(F32)[:, None], 0.0), axis=0, keepdims=True
    )
    scratch = scratch_of(s)
    vmem = pl.BlockSpec(memory_space=pltpu.VMEM)
    out_c, out_v = pl.pallas_call(
        functools.partial(kernel, s, tuple(scratch)),
        out_shape=(
            jax.ShapeDtypeStruct((s.outs, s.features), BF16),
            jax.ShapeDtypeStruct((1, 128), F32),
        ),
        in_specs=[vmem, vmem, vmem, pl.BlockSpec(memory_space=pltpu.SMEM)],
        out_specs=(vmem, vmem),
        scratch_shapes=list(scratch.values()),
        compiler_params=pltpu.CompilerParams(
            collective_id=0, has_side_effects=True, vmem_limit_bytes=48 * 1024 * 1024
        ),
    )(embeddings, lab, qr, pos)
    return out_c, out_v[0, : s.rows]


def build(mesh, y, x):
    z = mesh.shape["dp"] // 2

    def run(embeddings, outcomes, seed_index):
        devices = mesh.shape["dp"] * mesh.shape["cent"]
        s = Sizes(
            z, y, x, embeddings.shape[0] // devices, embeddings.shape[1],
            seed_index.shape[0] // mesh.shape["cent"],
        )
        return jax.shard_map(
            functools.partial(per_device, s),
            mesh=mesh,
            in_specs=(P(("dp", "cent"), None), P(("dp", "cent")), P("cent")),
            out_specs=(P(("cent", "dp"), None), P(("dp", "cent"))),
            check_vma=False,
        )(embeddings, outcomes, seed_index)

    return run


def solution(mesh):
    return build(mesh, mesh.shape["cent"] // 4, 4)
```

```python
import functools

import jax
import jax.numpy as jnp
from jax import lax
from jax.experimental import pallas as pl
from jax.experimental.pallas import tpu as pltpu
from jax.sharding import PartitionSpec as P

INVERSE_TEMP = 8.0
PSEUDO_COUNT = 1.0
ABSENT = -1e30
MESH = pl.DeviceIdType.MESH
F32 = jnp.float32
BF16 = jnp.bfloat16


class Sizes:
    def __init__(self, z, y, x, rows, features, seeds):
        self.z, self.y, self.x = z, y, x
        self.rows = rows
        self.chip = 2 * rows
        self.features = features
        self.half = features // 2
        self.slab = features // z
        self.local = (z // 2) * self.chip
        self.group = y * x * self.chip
        self.width = x * self.chip
        self.span = -(-self.width // 128) * 128
        self.seeds = seeds
        self.outs = seeds // (2 * z)
        self.lanes = -(-self.local // 128) * 128


def scratch_of(s):
    dma = pltpu.SemaphoreType.DMA
    v = pltpu.VMEM
    return dict(
        mine=v((32, s.features), BF16),
        theirs=v((32, s.features), BF16),
        block=v((s.chip, s.features), BF16),
        rows=v((s.y, s.x, s.chip, s.features), BF16),
        cents=v((2, s.local, s.features), BF16),
        lab_x=v((2, s.x, 1, s.span), F32),
        lab_y=v((s.y, 1, s.span), F32),
        cnt_s=v((s.x, s.y, s.lanes), F32),
        cnt_x=v((s.x, s.y, s.lanes), F32),
        cnt_t=v((s.y, 1, s.lanes), F32),
        cnt_y=v((s.y, 1, s.lanes), F32),
        logits=v((s.y, s.local, s.width), F32),
        probs=v((s.y, s.local, s.width), BF16),
        st_s=v((3, s.y, 1, s.span), F32),
        st_x=v((3, 2, s.x, s.y, 1, s.span), F32),
        st_t=v((3, s.y, 1, s.span), F32),
        st_y=v((3, s.y, s.y, 1, s.span), F32),
        st_f=v((3, s.y, 1, s.span), F32),
        mw_s=v((2, 8, s.lanes), F32),
        mw_r=v((2, s.z, 8, s.lanes), F32),
        num_s=v((2, s.z, s.local, s.slab), BF16),
        num_r=v((2, s.z, s.local, s.slab), BF16),
        table=v((2, s.y, s.x, s.local, s.slab), BF16),
        wide=v((2 * s.y * s.x * s.local, s.slab), F32),
        picked=v((s.outs, s.slab), F32),
        out_s=v((s.z, s.outs, s.slab), BF16),
        out_r=v((s.z, s.outs, s.slab), BF16),
        core_sem=dma((2,)),
        share_sem=dma((2, 2, s.y)),
        a1_sem=dma((2, 2, s.x)),
        a2_sem=dma((2, 2, s.y)),
        b1_sem=dma((2, 2, 2 * s.y)),
        b2_sem=dma((2, 2, 2 * s.y * s.x)),
        cent_sem=dma((2, s.z)),
        lab_sem=dma((2, 2 * s.x)),
        laby_sem=dma((2, s.y)),
        cnt_sem=dma((2, s.x)),
        cnty_sem=dma((2, s.y)),
        stx_sem=dma((3, 2, 2 * s.x)),
        sty_sem=dma((3, 2, s.y)),
        mw_sem=dma((2, 2, s.z)),
        num_sem=dma((2, 2, 3 * s.z)),
        new_sem=dma((2, 2 * s.z)),
        out_sem=dma((2, s.z)),
    )


def kernel(s, names, emb, lab, qr, pos, out_c, out_v, *scratch):
    ref = dict(zip(names, scratch))
    dp, cent = lax.axis_index("dp"), lax.axis_index("cent")
    z, core = dp // 2, dp % 2
    y, x = cent // s.x, cent % s.x

    def device(z_, core_, y_, x_):
        return (z_ * 2 + core_, y_ * s.x + x_)

    to_z = lambda p: device(p, core, y, x)
    to_y = lambda p: device(z, core, p, x)
    to_x = lambda p: device(z, core, y, p)
    to_cx = lambda p: device(z, p // s.x, y, p % s.x)
    partner = device(z, 1 - core, y, x)
    cx = core * s.x + x

    def each(n, me, do):
        def step(i, carry):
            do(lax.rem(me + i, n))
            return carry

        lax.fori_loop(1, n, step, 0)

    def copy(src, dst, sems, out_index, in_index, to):
        return pltpu.make_async_remote_copy(
            src_ref=src,
            dst_ref=dst,
            send_sem=sems.at[0, out_index],
            recv_sem=sems.at[1, in_index],
            device_id=to,
            device_id_type=MESH,
        )

    pending = []

    class Exchange:
        def __init__(self, n, me, to, sems, src, dst):
            self.n, self.me, self.to, self.sems, self.src, self.dst = n, me, to, sems, src, dst

        def start(self):
            each(self.n, self.me, lambda p: copy(
                self.src(p), self.dst(self.me), self.sems, p, self.me, self.to(p)).start())
            pending.append(self)

        def arrived(self):
            each(self.n, self.me, lambda p: copy(
                self.src(p), self.dst(p), self.sems, p, p, self.to(p)).wait_recv())

        def sent(self):
            each(self.n, self.me, lambda p: copy(
                self.src(p), self.dst(self.me), self.sems, p, self.me, self.to(p)).wait_send())

    barrier = pltpu.get_barrier_semaphore()

    def greet(to):
        return lambda p: pl.semaphore_signal(barrier, inc=1, device_id=to(p), device_id_type=MESH)

    each(2 * s.x, cx, greet(to_cx))
    each(s.y, y, greet(to_y))
    each(s.z, z, greet(to_z))
    pl.semaphore_wait(barrier, 2 * s.x - 1 + s.y - 1 + s.z - 1)

    mine, theirs = ref["mine"], ref["theirs"]
    mine[...] = jnp.concatenate(
        [emb[...].astype(F32), jnp.zeros((32 - s.rows, s.features), F32)], axis=0
    ).astype(BF16)
    swap = pltpu.make_async_remote_copy(
        src_ref=mine, dst_ref=theirs, send_sem=ref["core_sem"].at[0],
        recv_sem=ref["core_sem"].at[1], device_id=partner, device_id_type=MESH,
    )
    swap.start()

    lab_x = ref["lab_x"]
    lab_x[core, x] = lab[...]
    swap.wait_recv()
    rows, block = ref["rows"], ref["block"]
    own = mine[...].astype(F32)[: s.rows]
    other = theirs[...].astype(F32)[: s.rows]
    first = jnp.where(core == 0, own, other)
    second = jnp.where(core == 0, other, own)
    block[...] = jnp.concatenate([first, second], axis=0).astype(BF16)

    def near_first(j):
        far = (j + 1) // 2
        return lax.rem(y + jnp.where(j % 2 == 1, far, s.y - far), s.y)

    class Plane:
        def __init__(self, t, at, row, use):
            self.at, self.row, self.use = at, row, use
            self.sems = {name: ref[name + "_sem"].at[t] for name in ("share", "a1", "a2", "b1", "b2")}

        def a1(self, p, source):
            piece = self.at(y, source, 0)
            return copy(piece, piece, self.sems["a1"], p, source, to_x(p))

        def a2(self, p, source):
            piece = self.at(source, everything, 0)
            return copy(piece, piece, self.sems["a2"], p, source, to_y(p))

        def b1(self, k, p, source):
            piece = self.at(source, x, k)
            first = (k - 1) * s.y
            return copy(piece, piece, self.sems["b1"], first + p, first + source, to_y(p))

        def b2(self, k, yy, p, source):
            piece = self.at(yy, source, k)
            first = ((k - 1) * s.y + yy) * s.x
            return copy(piece, piece, self.sems["b2"], first + p, first + source, to_x(p))

        def share(self, yy, side):
            piece = self.row(yy, side)
            return copy(piece, piece, self.sems["share"], yy, yy, partner)

        def along_y(self, do):
            def step(j, carry):
                do(near_first(j))
                return carry

            lax.fori_loop(1, s.y, step, 0)

        def start_a(self):
            each(s.x, x, lambda p: self.a1(p, x).start())

        def start_b(self, k):
            self.along_y(lambda p: self.b1(k, p, y).start())
            each(s.x, x, lambda p: self.b2(k, y, p, x).start())

        def sent(self):
            each(s.x, x, lambda p: self.a1(p, x).wait_send())
            self.along_y(lambda p: self.a2(p, y).wait_send())
            for k in (1, 2):
                self.along_y(lambda p: self.b1(k, p, y).wait_send())

            def step(yy, carry):
                for k in (1, 2):
                    each(s.x, x, lambda p: self.b2(k, yy, p, x).wait_send())
                self.share(yy, core).wait_send()
                return carry

            lax.fori_loop(0, s.y, step, 0)

        def spread(self, k, low, high):
            def step(j, carry):
                source = near_first(j)
                self.b1(k, source, source).wait_recv()
                each(s.x, x, lambda p: self.b2(k, source, p, x).start())
                return carry

            lax.fori_loop(low, high, step, 0)

        def turn(self):
            each(s.x, x, lambda p: self.a1(p, p).wait_recv())
            self.along_y(lambda p: self.a2(p, y).start())

        def finish(self):
            def step(j, carry):
                @pl.when(j < s.y)
                def _():
                    source = near_first(j)

                    @pl.when(j > 0)
                    def _():
                        self.a2(source, source).wait_recv()

                    for k in (1, 2):
                        each(s.x, x, lambda p: self.b2(k, source, p, p).wait_recv())
                    self.share(source, core).start()

                @pl.when(j > 0)
                def _():
                    source = near_first(j - 1)
                    self.share(source, 1 - core).wait_recv()
                    self.use(source)

                return carry

            lax.fori_loop(0, s.y + 1, step, 0)

    def lanes_of(c):
        return pl.ds(pl.multiple_of(c * s.half, 128), s.half)

    logits, probs = ref["logits"], ref["probs"]
    cents = ref["cents"]
    everything = slice(None)

    def rows_of(b, lanes):
        return rows[b, :, :, lanes].reshape(s.width, -1)

    def products_of(t):
        def use(b):
            logits[b] = lax.dot_general(
                cents[t], rows_of(b, everything), (((1,), (1,)), ((), ())), preferred_element_type=F32
            )

        return use

    rows[y, x, :, lanes_of(core)] = block[:, lanes_of(core)]
    quarter = s.half // 4
    row_parts = ((0, quarter), (quarter, s.half - 2 * quarter), (s.half - quarter, quarter))

    def rows_at(yy, xx, k):
        start, size = row_parts[k]
        return rows.at[yy, xx, :, pl.ds(pl.multiple_of(core * s.half + start, 128), size)]

    gather = Plane(0, rows_at, lambda yy, c: rows.at[yy, :, :, lanes_of(c)], products_of(0))
    pending.append(gather)
    gather.start_a()
    gather.start_b(1)
    gather.start_b(2)

    zh = s.z // 2

    def cent_copy(src_z, to):
        place = pl.ds(pl.multiple_of((src_z % zh) * s.chip, 16), s.chip)
        return copy(block, cents.at[0, place, :], ref["cent_sem"], to, src_z, to_z(to))

    @pl.when(z // zh == core)
    def _():
        each(s.z, z, lambda p: cent_copy(z, p).start())
        cents[0, pl.ds(pl.multiple_of((z % zh) * s.chip, 16), s.chip), :] = block[...]

    lab_ex = Exchange(2 * s.x, cx, to_cx, ref["lab_sem"],
                      lambda p: lab_x.at[core, x], lambda p: lab_x.at[p // s.x, p % s.x])
    lab_ex.start()

    cnt_s, cnt_x = ref["cnt_s"], ref["cnt_x"]
    places = lax.broadcasted_iota(jnp.int32, (s.lanes, s.seeds), 0)
    hot_r = jnp.where(places == qr[1:2, :], 1.0, 0.0).astype(BF16)
    for xx in range(s.x):
        owner = lax.broadcasted_iota(jnp.int32, (s.y, s.seeds), 0) * s.x + (xx + core * s.x * s.y)
        hot_q = jnp.where(owner == qr[0:1, :], 1.0, 0.0).astype(BF16)
        cnt_s[xx] = lax.dot_general(hot_q, hot_r, (((1,), (1,)), ((), ())), preferred_element_type=F32)
    cnt_ex = Exchange(s.x, x, to_x, ref["cnt_sem"], lambda p: cnt_s.at[p], lambda p: cnt_x.at[p])
    cnt_ex.start()
    gather.spread(1, 1, s.y)
    gather.turn()

    cnt_ex.arrived()
    cnt_x[x] = cnt_s[x]
    total = cnt_x[0]
    for xx in range(1, s.x):
        total = total + cnt_x[xx]
    cnt_t, cnt_y = ref["cnt_t"], ref["cnt_y"]
    for yy in range(s.y):
        cnt_t[yy] = total[yy : yy + 1]
    cnty_ex = Exchange(s.y, y, to_y, ref["cnty_sem"], lambda p: cnt_t.at[p], lambda p: cnt_y.at[p])
    cnty_ex.start()
    lab_ex.arrived()
    lab_y = ref["lab_y"]
    line = lab_x[0, 0]
    for i in range(1, 2 * s.x):
        line = line + lab_x[i // s.x, i % s.x]
    lab_y[y] = line
    laby_ex = Exchange(s.y, y, to_y, ref["laby_sem"], lambda p: lab_y.at[y], lambda p: lab_y.at[p])
    laby_ex.start()

    def cents_in(i, carry):
        src_z = core * zh + i

        @pl.when(src_z != z)
        def _():
            place = pl.ds(pl.multiple_of(i * s.chip, 16), s.chip)
            copy(block, cents.at[0, place, :], ref["cent_sem"], src_z, src_z, to_z(src_z)).wait_recv()

        return carry

    gather.spread(2, 1, s.y)
    lax.fori_loop(0, zh, cents_in, 0)
    gather.finish()

    def to_column(row):
        eye = lax.broadcasted_iota(jnp.int32, (s.local, s.lanes), 0) == lax.broadcasted_iota(
            jnp.int32, (s.local, s.lanes), 1
        )
        return jnp.sum(jnp.where(eye, row, 0.0), axis=1, keepdims=True)

    cnty_ex.arrived()
    cnt_y[y] = cnt_t[y]
    line = cnt_y[0]
    for yy in range(1, s.y):
        line = line + cnt_y[yy]
    weight = to_column(line)
    laby_ex.arrived()

    @pl.when(z // zh == core)
    def _():
        each(s.z, z, lambda p: cent_copy(z, p).wait_send())

    ref["st_s"][...] = jnp.zeros_like(ref["st_s"])

    def blocks(do):
        def step(b, carry):
            do(2 * b)
            do(2 * b + 1)
            return carry

        lax.fori_loop(0, s.y // 2, step, 0)

    def lse_of(parts):
        top = functools.reduce(jnp.maximum, parts)
        return top + jnp.log(sum(jnp.exp(part - top) for part in parts))

    def total_of(parts):
        return sum(parts)

    def all_reduce(t, combine):
        st_s, st_x, st_t, st_y = (ref[name].at[t] for name in ("st_s", "st_x", "st_t", "st_y"))
        near = Exchange(2 * s.x, cx, to_cx, ref["stx_sem"].at[t], lambda p: st_s, lambda p: st_x.at[p // s.x, p % s.x])
        far = Exchange(s.y, y, to_y, ref["sty_sem"].at[t], lambda p: st_t, lambda p: st_y.at[p])
        near.start()
        yield
        near.arrived()
        st_x[core, x] = st_s[...]
        st_t[...] = combine([st_x[i // s.x, i % s.x] for i in range(2 * s.x)])
        far.start()
        yield
        far.arrived()
        st_y[y] = st_t[...]
        ref["st_f"][t] = combine([st_y[i] for i in range(s.y)])

    table, wide = ref["table"], ref["wide"]

    def widen(yy):
        size = s.x * s.local
        for a in range(2):
            wide[pl.ds(pl.multiple_of((a * s.y + yy) * size, 16), size), :] = (
                table[a, yy].reshape(size, s.slab).astype(F32)
            )

    low = max(16, s.local // 6 // 16 * 16)
    rest = (s.local - low) // 32 * 16
    new_parts = ((0, rest), (rest, s.local - low - rest), (s.local - low, low))

    def table_at(yy, xx, k):
        start, size = new_parts[(k + 2) % 3]
        return table.at[core, yy, xx, pl.ds(start, size), :]

    gather = Plane(1, table_at, lambda yy, c: table.at[c, yy], widen)
    pending.append(gather)

    for t in range(2):
        held = cents.at[t]
        exact = held[...].astype(F32)
        norm = jnp.sum(exact * exact, axis=1, keepdims=True)
        bias = jnp.where(weight > 0.0, (-0.5 * INVERSE_TEMP) * norm, ABSENT)
        st_s = ref["st_s"].at[t]

        if t == 1:
            blocks(products_of(1))

        def scores_of(b):
            value = jnp.where(weight > 0.0, INVERSE_TEMP * logits[b] + bias, ABSENT)
            logits[b] = value
            top = jnp.max(value, axis=0, keepdims=True)
            mass = jnp.sum(weight * jnp.exp(value - top), axis=0, keepdims=True)
            st_s[b, :, : s.width] = jnp.maximum(top + jnp.log(mass), ABSENT)

        blocks(scores_of)
        for _ in all_reduce(t, lse_of):
            pass
        norm_of = ref["st_f"].at[t]
        mw_s, mw_r = ref["mw_s"].at[t], ref["mw_r"].at[t]
        mw_s[...] = jnp.zeros_like(mw_s)

        def shares_of(b):
            value = jnp.exp(logits[b] - norm_of[b, :, : s.width])
            if t == 1:
                logits[b] = value
            rounded = value.astype(BF16)
            probs[b] = rounded
            label = lab_y[b, :, : s.width]
            line = lax.broadcasted_iota(jnp.int32, (8, s.width), 0)
            left = jnp.where(line == 0, 1.0, jnp.where(line == 1, label, 0.0)).astype(BF16)
            both = lax.dot_general(left, rounded, (((1,), (1,)), ((), ())), preferred_element_type=F32)
            mw_s[:, : s.local] += both

        blocks(shares_of)
        mw_ex = Exchange(s.z, z, to_z, ref["mw_sem"].at[t], lambda p: mw_s, lambda p: mw_r.at[p])
        mw_ex.start()

        num_s, num_r = ref["num_s"].at[t], ref["num_r"].at[t]
        half = s.local // 2
        parts = ((0, half), (half, half)) if t == 0 else new_parts

        def num_copy(k, p, source):
            piece = pl.ds(parts[k][0], parts[k][1])
            return copy(num_s.at[p, piece, :], num_r.at[source, piece, :], ref["num_sem"].at[t],
                        k * s.z + p, k * s.z + source, to_z(p))

        pairs = s.z // 2

        def numer_of(i, carry):
            pair = lax.rem(z // 2 + 1 + i, pairs)
            lanes = pl.ds(pl.multiple_of(pair * 2 * s.slab, 128), 2 * s.slab)
            acc = jnp.zeros((s.local, 2 * s.slab), F32)
            for b in range(s.y):
                acc = acc + jnp.dot(probs[b], rows_of(b, lanes), preferred_element_type=F32)
            for side in range(2):
                p = pair * 2 + side
                num_s[p] = acc[:, side * s.slab : (side + 1) * s.slab].astype(BF16)

                @pl.when(p != z)
                def _():
                    num_copy(0, p, z).start()

            return carry

        lax.fori_loop(0, pairs, numer_of, 0)
        for k in range(1, len(parts)):
            each(s.z, z, lambda p: num_copy(k, p, z).start())
        mw_ex.arrived()
        mw_r[z] = mw_s[...]
        both = mw_r[0]
        for i in range(1, s.z):
            both = both + mw_r[i]
        mass = to_column(both[0:1])
        if t == 1:
            wins = to_column(both[1:2])
            rate = weight * ((wins + 0.5 * PSEUDO_COUNT) / (mass + PSEUDO_COUNT))
            sc = ref["st_s"].at[2]

            def step_scores(b):
                sc[b, :, : s.width] = jnp.sum(logits[b] * rate, axis=0, keepdims=True)

            blocks(step_scores)
            reduce_scores = all_reduce(2, total_of)
            next(reduce_scores)
        mylanes = pl.ds(pl.multiple_of(z * s.slab, 128), s.slab)

        def fresh(k):
            each(s.z, z, lambda p: num_copy(k, p, p).wait_recv())
            first, size = parts[k]
            piece = slice(first, first + size)
            num_r[z, piece, :] = num_s[z, piece, :]
            acc = num_r[0, piece, :].astype(F32)
            for i in range(1, s.z):
                acc = acc + num_r[i, piece, :].astype(F32)
            acc = acc + PSEUDO_COUNT * held[piece, mylanes].astype(F32)
            return (acc / (mass[piece] + PSEUDO_COUNT)).astype(BF16)

        if t == 0:
            def new_copy(k, p, source):
                lanes = pl.ds(pl.multiple_of(source * s.slab, 128), s.slab)
                piece = cents.at[1, pl.ds(parts[k][0], parts[k][1]), lanes]
                return copy(piece, piece, ref["new_sem"], k * s.z + p, k * s.z + source, to_z(p))

            for k in range(2):
                cents[1, parts[k][0] : parts[k][0] + parts[k][1], mylanes] = fresh(k)
                each(s.z, z, lambda p: new_copy(k, p, z).start())
            for k in range(2):
                each(s.z, z, lambda p: new_copy(k, p, p).wait_recv())
        else:
            for k in range(3):
                table[core, y, x, parts[k][0] : parts[k][0] + parts[k][1], :] = fresh(k)
                if k < 2:
                    gather.start_b(k + 1)
                else:
                    gather.start_a()
            for k in range(3):
                each(s.z, z, lambda p: num_copy(k, p, z).wait_send())
        if t == 0:
            for k in range(2):
                each(s.z, z, lambda p: num_copy(k, p, z).wait_send())
                each(s.z, z, lambda p: new_copy(k, p, z).wait_send())

    next(reduce_scores)
    gather.spread(1, 1, s.y)
    gather.turn()
    gather.spread(2, 1, s.y)
    for _ in reduce_scores:
        pass
    gather.finish()
    final = ref["st_f"]
    offset = x * s.chip + core * s.rows
    n_out = 32
    here = lax.broadcasted_iota(jnp.int32, (n_out, s.span), 1)
    wanted = lax.broadcasted_iota(jnp.int32, (n_out, s.span), 0) + offset
    column = jnp.sum(jnp.where(here == wanted, final[2, y], 0.0), axis=1, keepdims=True)
    eye = lax.broadcasted_iota(jnp.int32, (n_out, 128), 0) == lax.broadcasted_iota(jnp.int32, (n_out, 128), 1)
    out_v[...] = jnp.sum(jnp.where(eye, column, 0.0), axis=0, keepdims=True)

    picked, out_s, out_r = ref["picked"], ref["out_s"], ref["out_r"]
    out_ex = Exchange(s.z, z, to_z, ref["out_sem"], lambda p: out_s.at[p], lambda p: out_r.at[p])

    def pick(i, carry):
        p = lax.rem(z + 1 + i, s.z)
        base = (2 * p + core) * s.outs

        def eight(j, carry):
            for k in range(8):
                n = j * 8 + k
                picked[pl.ds(n, 1), :] = wide[pl.ds(pos[base + n], 1), :]
            return carry

        lax.fori_loop(0, s.outs // 8, eight, 0)
        out_s[p] = picked[...].astype(BF16)

        @pl.when(p != z)
        def _():
            copy(out_s.at[p], out_r.at[z], ref["out_sem"], p, z, to_z(p)).start()

        return carry

    lax.fori_loop(0, s.z, pick, 0)
    pending.append(out_ex)
    out_ex.arrived()
    out_r[z] = out_s[z]
    for i in range(s.z):
        out_c[:, i * s.slab : (i + 1) * s.slab] = out_r[i]
    swap.wait_send()
    for exchange in pending:
        exchange.sent()


def per_device(s, embeddings, outcomes, seed_index):
    core = lax.axis_index("dp") % 2
    cent = lax.axis_index("cent")
    plane = s.rows * s.x * s.y
    dp, rest = seed_index // plane, seed_index % plane
    zs, side = dp // 2, dp % 2
    zh = s.z // 2
    q = (zs // zh) * (s.x * s.y) + rest // s.rows
    r = (zs % zh) * s.chip + side * s.rows + rest % s.rows
    qr = jnp.stack([q, r])
    pos = q * s.local + r
    offset = (cent % s.x) * s.chip + core * s.rows
    spot = lax.broadcasted_iota(jnp.int32, (s.rows, s.span), 1) - lax.broadcasted_iota(
        jnp.int32, (s.rows, s.span), 0
    )
    lab = jnp.sum(
        jnp.where(spot == offset, outcomes.astype(F32)[:, None], 0.0), axis=0, keepdims=True
    )
    scratch = scratch_of(s)
    vmem = pl.BlockSpec(memory_space=pltpu.VMEM)
    out_c, out_v = pl.pallas_call(
        functools.partial(kernel, s, tuple(scratch)),
        out_shape=(
            jax.ShapeDtypeStruct((s.outs, s.features), BF16),
            jax.ShapeDtypeStruct((1, 128), F32),
        ),
        in_specs=[vmem, vmem, vmem, pl.BlockSpec(memory_space=pltpu.SMEM)],
        out_specs=(vmem, vmem),
        scratch_shapes=list(scratch.values()),
        compiler_params=pltpu.CompilerParams(
            collective_id=0, has_side_effects=True, vmem_limit_bytes=48 * 1024 * 1024
        ),
    )(embeddings, lab, qr, pos)
    return out_c, out_v[0, : s.rows]


def build(mesh, y, x):
    z = mesh.shape["dp"] // 2

    def run(embeddings, outcomes, seed_index):
        devices = mesh.shape["dp"] * mesh.shape["cent"]
        s = Sizes(
            z, y, x, embeddings.shape[0] // devices, embeddings.shape[1],
            seed_index.shape[0] // mesh.shape["cent"],
        )
        return jax.shard_map(
            functools.partial(per_device, s),
            mesh=mesh,
            in_specs=(P(("dp", "cent"), None), P(("dp", "cent")), P("cent")),
            out_specs=(P(("cent", "dp"), None), P(("dp", "cent"))),
            check_vma=False,
        )(embeddings, outcomes, seed_index)

    return run


def solution(mesh):
    return build(mesh, mesh.shape["cent"] // 4, 4)
```

```python
import functools

import jax
import jax.numpy as jnp
from jax import lax
from jax.experimental import pallas as pl
from jax.experimental.pallas import tpu as pltpu
from jax.sharding import PartitionSpec as P

INVERSE_TEMP = 8.0
PSEUDO_COUNT = 1.0
ABSENT = -1e30
MESH = pl.DeviceIdType.MESH
F32 = jnp.float32
BF16 = jnp.bfloat16


class Sizes:
    def __init__(self, z, y, x, rows, features, seeds):
        self.z, self.y, self.x = z, y, x
        self.rows = rows
        self.chip = 2 * rows
        self.features = features
        self.half = features // 2
        self.slab = features // z
        self.local = (z // 2) * self.chip
        self.group = y * x * self.chip
        self.width = x * self.chip
        self.span = -(-self.width // 128) * 128
        self.seeds = seeds
        self.outs = seeds // (2 * z)
        self.lanes = -(-self.local // 128) * 128


def scratch_of(s):
    dma = pltpu.SemaphoreType.DMA
    v = pltpu.VMEM
    return dict(
        qr=v((2, s.seeds), jnp.int32),
        pos=pltpu.SMEM((s.seeds,), jnp.int32),
        score=v((1, 128), F32),
        in_sem=dma((4,)),
        store_sem=dma((s.z + 1,)),
        mine=v((32, s.features), BF16),
        theirs=v((32, s.features), BF16),
        block=v((s.chip, s.features), BF16),
        rows=v((s.y, s.x, s.chip, s.features), BF16),
        cents=v((2, s.local, s.features), BF16),
        lab_x=v((2, s.x, 1, s.span), F32),
        lab_y=v((s.y, 1, s.span), F32),
        cnt_s=v((s.x, s.y, s.lanes), F32),
        cnt_x=v((s.x, s.y, s.lanes), F32),
        cnt_t=v((s.y, 1, s.lanes), F32),
        cnt_y=v((s.y, 1, s.lanes), F32),
        logits=v((s.y, s.local, s.width), F32),
        tops=v((s.y, 1, s.width), F32),
        probs=v((s.y, s.local, s.width), BF16),
        st_s=v((3, s.y, 1, s.span), F32),
        st_x=v((3, 2, s.x, s.y, 1, s.span), F32),
        st_t=v((3, s.y, 1, s.span), F32),
        st_y=v((3, s.y, s.y, 1, s.span), F32),
        st_f=v((3, s.y, 1, s.span), F32),
        mw_s=v((2, 8, s.lanes), F32),
        mw_r=v((2, s.z, 8, s.lanes), F32),
        num_s=v((2, s.z, s.local, s.slab), BF16),
        num_r=v((2, s.z, s.local, s.slab), BF16),
        table=v((2, s.y, s.x, s.local, s.slab), BF16),
        wide=v((2 * s.y * s.x * s.local, s.slab), F32),
        picked=v((s.outs, s.slab), F32),
        out_s=v((s.z, s.outs, s.slab), BF16),
        out_r=v((s.z, s.outs, s.slab), BF16),
        core_sem=dma((2,)),
        share_sem=dma((2, 2, s.y)),
        a1_sem=dma((2, 2, s.x)),
        a2_sem=dma((2, 2, s.y)),
        b1_sem=dma((2, 2, 2 * s.y)),
        b2_sem=dma((2, 2, 2 * s.y * s.x)),
        cent_sem=dma((2, s.z)),
        lab_sem=dma((2, 2 * s.x)),
        laby_sem=dma((2, s.y)),
        cnt_sem=dma((2, s.x)),
        cnty_sem=dma((2, s.y)),
        stx_sem=dma((3, 2, 2 * s.x)),
        sty_sem=dma((3, 2, s.y)),
        mw_sem=dma((2, 2, s.z)),
        num_sem=dma((2, 2, 3 * s.z)),
        new_sem=dma((2, 2 * s.z)),
        out_sem=dma((2, s.z)),
    )


def kernel(s, names, emb, lab, qr_in, pos_in, out_c, out_v, *scratch):
    ref = dict(zip(names, scratch))
    mine, theirs, qr, pos, lab_x = (ref[name] for name in ("mine", "theirs", "qr", "pos", "lab_x"))
    dp, cent = lax.axis_index("dp"), lax.axis_index("cent")
    z, core = dp // 2, dp % 2
    y, x = cent // s.x, cent % s.x

    def device(z_, core_, y_, x_):
        return (z_ * 2 + core_, y_ * s.x + x_)

    to_z = lambda p: device(p, core, y, x)
    to_y = lambda p: device(z, core, p, x)
    to_x = lambda p: device(z, core, y, p)
    to_cx = lambda p: device(z, p // s.x, y, p % s.x)
    partner = device(z, 1 - core, y, x)
    cx = core * s.x + x

    def each(n, me, do):
        def step(i, carry):
            do(lax.rem(me + i, n))
            return carry

        lax.fori_loop(1, n, step, 0)

    def copy(src, dst, sems, out_index, in_index, to):
        return pltpu.make_async_remote_copy(
            src_ref=src,
            dst_ref=dst,
            send_sem=sems.at[0, out_index],
            recv_sem=sems.at[1, in_index],
            device_id=to,
            device_id_type=MESH,
        )

    pending = []

    class Exchange:
        def __init__(self, n, me, to, sems, src, dst):
            self.n, self.me, self.to, self.sems, self.src, self.dst = n, me, to, sems, src, dst

        def start(self):
            each(self.n, self.me, lambda p: copy(
                self.src(p), self.dst(self.me), self.sems, p, self.me, self.to(p)).start())
            pending.append(self)

        def arrived(self):
            each(self.n, self.me, lambda p: copy(
                self.src(p), self.dst(p), self.sems, p, p, self.to(p)).wait_recv())

        def sent(self):
            each(self.n, self.me, lambda p: copy(
                self.src(p), self.dst(self.me), self.sems, p, self.me, self.to(p)).wait_send())

    loads = [
        pltpu.make_async_copy(src, dst, ref["in_sem"].at[i])
        for i, (src, dst) in enumerate(((emb, mine), (lab, lab_x.at[core, x]), (qr_in, qr), (pos_in, pos)))
    ]
    for load in loads:
        load.start()
    barrier = pltpu.get_barrier_semaphore()

    def greet(to):
        return lambda p: pl.semaphore_signal(barrier, inc=1, device_id=to(p), device_id_type=MESH)

    each(2 * s.x, cx, greet(to_cx))
    each(s.y, y, greet(to_y))
    each(s.z, z, greet(to_z))
    pl.semaphore_wait(barrier, 2 * s.x - 1 + s.y - 1 + s.z - 1)

    loads[0].wait()
    swap = pltpu.make_async_remote_copy(
        src_ref=mine, dst_ref=theirs, send_sem=ref["core_sem"].at[0],
        recv_sem=ref["core_sem"].at[1], device_id=partner, device_id_type=MESH,
    )
    swap.start()

    swap.wait_recv()
    rows, block = ref["rows"], ref["block"]
    own = mine[...].astype(F32)[: s.rows]
    other = theirs[...].astype(F32)[: s.rows]
    first = jnp.where(core == 0, own, other)
    second = jnp.where(core == 0, other, own)
    block[...] = jnp.concatenate([first, second], axis=0).astype(BF16)

    def near_first(j):
        far = (j + 1) // 2
        return lax.rem(y + jnp.where(j % 2 == 1, far, s.y - far), s.y)

    class Plane:
        def __init__(self, t, at, row, use):
            self.at, self.row, self.use = at, row, use
            self.sems = {name: ref[name + "_sem"].at[t] for name in ("share", "a1", "a2", "b1", "b2")}

        def a1(self, p, source):
            piece = self.at(y, source, 0)
            return copy(piece, piece, self.sems["a1"], p, source, to_x(p))

        def a2(self, p, source):
            piece = self.at(source, everything, 0)
            return copy(piece, piece, self.sems["a2"], p, source, to_y(p))

        def b1(self, k, p, source):
            piece = self.at(source, x, k)
            first = (k - 1) * s.y
            return copy(piece, piece, self.sems["b1"], first + p, first + source, to_y(p))

        def b2(self, k, yy, p, source):
            piece = self.at(yy, source, k)
            first = ((k - 1) * s.y + yy) * s.x
            return copy(piece, piece, self.sems["b2"], first + p, first + source, to_x(p))

        def share(self, yy, side):
            piece = self.row(yy, side)
            return copy(piece, piece, self.sems["share"], yy, yy, partner)

        def along_y(self, do):
            def step(j, carry):
                do(near_first(j))
                return carry

            lax.fori_loop(1, s.y, step, 0)

        def start_a(self):
            each(s.x, x, lambda p: self.a1(p, x).start())

        def start_b(self, k):
            self.along_y(lambda p: self.b1(k, p, y).start())
            each(s.x, x, lambda p: self.b2(k, y, p, x).start())

        def sent(self):
            each(s.x, x, lambda p: self.a1(p, x).wait_send())
            self.along_y(lambda p: self.a2(p, y).wait_send())
            for k in (1, 2):
                self.along_y(lambda p: self.b1(k, p, y).wait_send())

            def step(yy, carry):
                for k in (1, 2):
                    each(s.x, x, lambda p: self.b2(k, yy, p, x).wait_send())
                self.share(yy, core).wait_send()
                return carry

            lax.fori_loop(0, s.y, step, 0)

        def spread(self, k, low, high):
            def step(j, carry):
                source = near_first(j)
                self.b1(k, source, source).wait_recv()
                each(s.x, x, lambda p: self.b2(k, source, p, x).start())
                return carry

            lax.fori_loop(low, high, step, 0)

        def turn(self):
            each(s.x, x, lambda p: self.a1(p, p).wait_recv())
            self.along_y(lambda p: self.a2(p, y).start())

        def finish(self):
            def step(j, carry):
                @pl.when(j < s.y)
                def _():
                    source = near_first(j)

                    @pl.when(j > 0)
                    def _():
                        self.a2(source, source).wait_recv()

                    for k in (1, 2):
                        each(s.x, x, lambda p: self.b2(k, source, p, p).wait_recv())
                    self.share(source, core).start()

                @pl.when(j > 0)
                def _():
                    source = near_first(j - 1)
                    self.share(source, 1 - core).wait_recv()
                    self.use(source)

                return carry

            lax.fori_loop(0, s.y + 1, step, 0)

    def lanes_of(c):
        return pl.ds(pl.multiple_of(c * s.half, 128), s.half)

    logits, probs, tops = ref["logits"], ref["probs"], ref["tops"]
    cents = ref["cents"]
    everything = slice(None)

    def rows_of(b, lanes):
        return rows[b, :, :, lanes].reshape(s.width, -1)

    def products_of(t):
        def use(b):
            logits[b] = lax.dot_general(
                cents[t], rows_of(b, everything), (((1,), (1,)), ((), ())), preferred_element_type=F32
            )

        return use

    rows[y, x, :, lanes_of(core)] = block[:, lanes_of(core)]
    quarter = s.half // 4
    row_parts = ((0, quarter), (quarter, s.half - 2 * quarter), (s.half - quarter, quarter))

    def rows_at(yy, xx, k):
        start, size = row_parts[k]
        return rows.at[yy, xx, :, pl.ds(pl.multiple_of(core * s.half + start, 128), size)]

    gather = Plane(0, rows_at, lambda yy, c: rows.at[yy, :, :, lanes_of(c)], products_of(0))
    pending.append(gather)
    gather.start_a()
    gather.start_b(1)
    gather.start_b(2)

    zh = s.z // 2

    def cent_copy(src_z, to):
        place = pl.ds(pl.multiple_of((src_z % zh) * s.chip, 16), s.chip)
        return copy(block, cents.at[0, place, :], ref["cent_sem"], to, src_z, to_z(to))

    @pl.when(z // zh == core)
    def _():
        each(s.z, z, lambda p: cent_copy(z, p).start())
        cents[0, pl.ds(pl.multiple_of((z % zh) * s.chip, 16), s.chip), :] = block[...]

    lab_ex = Exchange(2 * s.x, cx, to_cx, ref["lab_sem"],
                      lambda p: lab_x.at[core, x], lambda p: lab_x.at[p // s.x, p % s.x])
    loads[1].wait()
    lab_ex.start()
    loads[2].wait()
    loads[3].wait()

    cnt_s, cnt_x = ref["cnt_s"], ref["cnt_x"]
    places = lax.broadcasted_iota(jnp.int32, (s.lanes, s.seeds), 0)
    hot_r = jnp.where(places == qr[1:2, :], 1.0, 0.0).astype(BF16)
    for xx in range(s.x):
        owner = lax.broadcasted_iota(jnp.int32, (s.y, s.seeds), 0) * s.x + (xx + core * s.x * s.y)
        hot_q = jnp.where(owner == qr[0:1, :], 1.0, 0.0).astype(BF16)
        cnt_s[xx] = lax.dot_general(hot_q, hot_r, (((1,), (1,)), ((), ())), preferred_element_type=F32)
    cnt_ex = Exchange(s.x, x, to_x, ref["cnt_sem"], lambda p: cnt_s.at[p], lambda p: cnt_x.at[p])
    cnt_ex.start()
    gather.spread(1, 1, s.y)
    gather.turn()

    cnt_ex.arrived()
    cnt_x[x] = cnt_s[x]
    total = cnt_x[0]
    for xx in range(1, s.x):
        total = total + cnt_x[xx]
    cnt_t, cnt_y = ref["cnt_t"], ref["cnt_y"]
    for yy in range(s.y):
        cnt_t[yy] = total[yy : yy + 1]
    cnty_ex = Exchange(s.y, y, to_y, ref["cnty_sem"], lambda p: cnt_t.at[p], lambda p: cnt_y.at[p])
    cnty_ex.start()
    lab_ex.arrived()
    lab_y = ref["lab_y"]
    line = lab_x[0, 0]
    for i in range(1, 2 * s.x):
        line = line + lab_x[i // s.x, i % s.x]
    lab_y[y] = line
    laby_ex = Exchange(s.y, y, to_y, ref["laby_sem"], lambda p: lab_y.at[y], lambda p: lab_y.at[p])
    laby_ex.start()

    def cents_in(i, carry):
        src_z = core * zh + i

        @pl.when(src_z != z)
        def _():
            place = pl.ds(pl.multiple_of(i * s.chip, 16), s.chip)
            copy(block, cents.at[0, place, :], ref["cent_sem"], src_z, src_z, to_z(src_z)).wait_recv()

        return carry

    gather.spread(2, 1, s.y)
    lax.fori_loop(0, zh, cents_in, 0)
    gather.finish()

    def to_column(row):
        eye = lax.broadcasted_iota(jnp.int32, (s.local, s.lanes), 0) == lax.broadcasted_iota(
            jnp.int32, (s.local, s.lanes), 1
        )
        return jnp.sum(jnp.where(eye, row, 0.0), axis=1, keepdims=True)

    cnty_ex.arrived()
    cnt_y[y] = cnt_t[y]
    line = cnt_y[0]
    for yy in range(1, s.y):
        line = line + cnt_y[yy]
    weight = to_column(line)
    laby_ex.arrived()

    @pl.when(z // zh == core)
    def _():
        each(s.z, z, lambda p: cent_copy(z, p).wait_send())

    ref["st_s"][...] = jnp.zeros_like(ref["st_s"])

    def blocks(do):
        def step(b, carry):
            do(2 * b)
            do(2 * b + 1)
            return carry

        lax.fori_loop(0, s.y // 2, step, 0)

    def lse_of(parts):
        top = functools.reduce(jnp.maximum, parts)
        return top + jnp.log(sum(jnp.exp(part - top) for part in parts))

    def total_of(parts):
        return sum(parts)

    def all_reduce(t, combine):
        st_s, st_x, st_t, st_y = (ref[name].at[t] for name in ("st_s", "st_x", "st_t", "st_y"))
        near = Exchange(2 * s.x, cx, to_cx, ref["stx_sem"].at[t], lambda p: st_s, lambda p: st_x.at[p // s.x, p % s.x])
        far = Exchange(s.y, y, to_y, ref["sty_sem"].at[t], lambda p: st_t, lambda p: st_y.at[p])
        near.start()
        yield
        near.arrived()
        st_x[core, x] = st_s[...]
        st_t[...] = combine([st_x[i // s.x, i % s.x] for i in range(2 * s.x)])
        far.start()
        yield
        far.arrived()
        st_y[y] = st_t[...]
        ref["st_f"][t] = combine([st_y[i] for i in range(s.y)])

    table, wide = ref["table"], ref["wide"]

    def widen(yy):
        size = s.x * s.local
        for a in range(2):
            wide[pl.ds(pl.multiple_of((a * s.y + yy) * size, 16), size), :] = (
                table[a, yy].reshape(size, s.slab).astype(F32)
            )

    low = 48
    rest = (s.local - low) // 32 * 16
    new_parts = ((0, rest), (rest, s.local - low - rest), (s.local - low, low))

    def table_at(yy, xx, k):
        start, size = new_parts[(k + 2) % 3]
        return table.at[core, yy, xx, pl.ds(start, size), :]

    gather = Plane(1, table_at, lambda yy, c: table.at[c, yy], widen)
    pending.append(gather)

    for t in range(2):
        held = cents.at[t]
        exact = held[...].astype(F32)
        norm = jnp.sum(exact * exact, axis=1, keepdims=True)
        bias = jnp.where(weight > 0.0, (-0.5 * INVERSE_TEMP) * norm, ABSENT)
        st_s = ref["st_s"].at[t]

        if t == 1:
            blocks(products_of(1))

        def scores_of(b):
            value = jnp.where(weight > 0.0, INVERSE_TEMP * logits[b] + bias, ABSENT)
            top = jnp.max(value, axis=0, keepdims=True)
            power = jnp.exp(value - top)
            logits[b] = power
            tops[b] = top
            mass = jnp.sum(weight * power, axis=0, keepdims=True)
            st_s[b, :, : s.width] = jnp.maximum(top + jnp.log(mass), ABSENT)

        blocks(scores_of)
        for _ in all_reduce(t, lse_of):
            pass
        norm_of = ref["st_f"].at[t]
        mw_s, mw_r = ref["mw_s"].at[t], ref["mw_r"].at[t]
        mw_s[...] = jnp.zeros_like(mw_s)

        def shares_of(b):
            value = logits[b] * jnp.exp(tops[b] - norm_of[b, :, : s.width])
            if t == 1:
                logits[b] = value
            rounded = value.astype(BF16)
            probs[b] = rounded
            label = lab_y[b, :, : s.width]
            line = lax.broadcasted_iota(jnp.int32, (8, s.width), 0)
            left = jnp.where(line == 0, 1.0, jnp.where(line == 1, label, 0.0)).astype(BF16)
            both = lax.dot_general(left, rounded, (((1,), (1,)), ((), ())), preferred_element_type=F32)
            mw_s[:, : s.local] += both

        blocks(shares_of)
        mw_ex = Exchange(s.z, z, to_z, ref["mw_sem"].at[t], lambda p: mw_s, lambda p: mw_r.at[p])
        mw_ex.start()

        num_s, num_r = ref["num_s"].at[t], ref["num_r"].at[t]
        half = s.local // 2
        parts = ((0, half), (half, half)) if t == 0 else new_parts

        def num_copy(k, p, source):
            piece = pl.ds(parts[k][0], parts[k][1])
            return copy(num_s.at[p, piece, :], num_r.at[source, piece, :], ref["num_sem"].at[t],
                        k * s.z + p, k * s.z + source, to_z(p))

        pairs = s.z // 2

        def numer_of(i, carry):
            pair = lax.rem(z // 2 + 1 + i, pairs)
            lanes = pl.ds(pl.multiple_of(pair * 2 * s.slab, 128), 2 * s.slab)
            acc = jnp.zeros((s.local, 2 * s.slab), F32)
            for b in range(s.y):
                acc = acc + jnp.dot(probs[b], rows_of(b, lanes), preferred_element_type=F32)
            for side in range(2):
                p = pair * 2 + side
                num_s[p] = acc[:, side * s.slab : (side + 1) * s.slab].astype(BF16)

                @pl.when(p != z)
                def _():
                    num_copy(0, p, z).start()

            return carry

        lax.fori_loop(0, pairs, numer_of, 0)
        for k in range(1, len(parts)):
            each(s.z, z, lambda p: num_copy(k, p, z).start())
        mw_ex.arrived()
        mw_r[z] = mw_s[...]
        both = mw_r[0]
        for i in range(1, s.z):
            both = both + mw_r[i]
        mass = to_column(both[0:1])
        if t == 1:
            wins = to_column(both[1:2])
            rate = weight * ((wins + 0.5 * PSEUDO_COUNT) / (mass + PSEUDO_COUNT))
            sc = ref["st_s"].at[2]

            def step_scores(b):
                sc[b, :, : s.width] = jnp.sum(logits[b] * rate, axis=0, keepdims=True)

            blocks(step_scores)
            reduce_scores = all_reduce(2, total_of)
            next(reduce_scores)
        mylanes = pl.ds(pl.multiple_of(z * s.slab, 128), s.slab)

        def fresh(k):
            each(s.z, z, lambda p: num_copy(k, p, p).wait_recv())
            first, size = parts[k]
            piece = slice(first, first + size)
            num_r[z, piece, :] = num_s[z, piece, :]
            acc = num_r[0, piece, :].astype(F32)
            for i in range(1, s.z):
                acc = acc + num_r[i, piece, :].astype(F32)
            acc = acc + PSEUDO_COUNT * held[piece, mylanes].astype(F32)
            return (acc / (mass[piece] + PSEUDO_COUNT)).astype(BF16)

        if t == 0:
            def new_copy(k, p, source):
                lanes = pl.ds(pl.multiple_of(source * s.slab, 128), s.slab)
                piece = cents.at[1, pl.ds(parts[k][0], parts[k][1]), lanes]
                return copy(piece, piece, ref["new_sem"], k * s.z + p, k * s.z + source, to_z(p))

            for k in range(2):
                cents[1, parts[k][0] : parts[k][0] + parts[k][1], mylanes] = fresh(k)
                each(s.z, z, lambda p: new_copy(k, p, z).start())
            for k in range(2):
                each(s.z, z, lambda p: new_copy(k, p, p).wait_recv())
        else:
            for k in range(3):
                table[core, y, x, parts[k][0] : parts[k][0] + parts[k][1], :] = fresh(k)
                if k < 2:
                    gather.start_b(k + 1)
                else:
                    gather.start_a()
            for k in range(3):
                each(s.z, z, lambda p: num_copy(k, p, z).wait_send())
        if t == 0:
            for k in range(2):
                each(s.z, z, lambda p: num_copy(k, p, z).wait_send())
                each(s.z, z, lambda p: new_copy(k, p, z).wait_send())

    next(reduce_scores)
    gather.spread(1, 1, s.y)
    gather.turn()
    gather.spread(2, 1, s.y)
    for _ in reduce_scores:
        pass
    final = ref["st_f"]
    offset = x * s.chip + core * s.rows
    n_out = 32
    here = lax.broadcasted_iota(jnp.int32, (n_out, s.span), 1)
    wanted = lax.broadcasted_iota(jnp.int32, (n_out, s.span), 0) + offset
    column = jnp.sum(jnp.where(here == wanted, final[2, y], 0.0), axis=1, keepdims=True)
    eye = lax.broadcasted_iota(jnp.int32, (n_out, 128), 0) == lax.broadcasted_iota(jnp.int32, (n_out, 128), 1)
    ref["score"][...] = jnp.sum(jnp.where(eye, column, 0.0), axis=0, keepdims=True)
    store_score = pltpu.make_async_copy(ref["score"], out_v, ref["store_sem"].at[s.z])
    store_score.start()
    gather.finish()
    picked, out_s, out_r = ref["picked"], ref["out_s"], ref["out_r"]
    out_ex = Exchange(s.z, z, to_z, ref["out_sem"], lambda p: out_s.at[p], lambda p: out_r.at[p])

    def pick(i, carry):
        p = lax.rem(z + 1 + i, s.z)
        base = (2 * p + core) * s.outs

        def eight(j, carry):
            for k in range(8):
                n = j * 8 + k
                picked[pl.ds(n, 1), :] = wide[pl.ds(pos[base + n], 1), :]
            return carry

        lax.fori_loop(0, s.outs // 8, eight, 0)
        out_s[p] = picked[...].astype(BF16)

        @pl.when(p != z)
        def _():
            copy(out_s.at[p], out_r.at[z], ref["out_sem"], p, z, to_z(p)).start()

        return carry

    lax.fori_loop(0, s.z, pick, 0)
    pending.append(out_ex)
    def store(p, block):
        lanes = pl.ds(pl.multiple_of(p * s.slab, 128), s.slab)
        return pltpu.make_async_copy(block, out_c.at[:, lanes], ref["store_sem"].at[p])

    store(z, out_s.at[z]).start()

    def keep(i, carry):
        p = lax.rem(z + s.z - i, s.z)
        copy(out_s.at[p], out_r.at[p], ref["out_sem"], p, p, to_z(p)).wait_recv()
        store(p, out_r.at[p]).start()
        return carry

    lax.fori_loop(1, s.z, keep, 0)
    swap.wait_send()
    for exchange in pending:
        exchange.sent()
    store_score.wait()
    store(z, out_s.at[z]).wait()
    each(s.z, z, lambda p: store(p, out_r.at[p]).wait())


def per_device(s, embeddings, outcomes, seed_index):
    core = lax.axis_index("dp") % 2
    cent = lax.axis_index("cent")
    plane = s.rows * s.x * s.y
    dp, rest = seed_index // plane, seed_index % plane
    zs, side = dp // 2, dp % 2
    zh = s.z // 2
    q = (zs // zh) * (s.x * s.y) + rest // s.rows
    r = (zs % zh) * s.chip + side * s.rows + rest % s.rows
    qr = jnp.stack([q, r])
    pos = q * s.local + r
    offset = (cent % s.x) * s.chip + core * s.rows
    spot = lax.broadcasted_iota(jnp.int32, (s.rows, s.span), 1) - lax.broadcasted_iota(
        jnp.int32, (s.rows, s.span), 0
    )
    lab = jnp.sum(
        jnp.where(spot == offset, outcomes.astype(F32)[:, None], 0.0), axis=0, keepdims=True
    )
    scratch = scratch_of(s)
    anywhere = pl.BlockSpec(memory_space=pl.ANY)
    padded = jnp.pad(embeddings, ((0, 32 - s.rows), (0, 0)))
    out_c, out_v = pl.pallas_call(
        functools.partial(kernel, s, tuple(scratch)),
        out_shape=(
            jax.ShapeDtypeStruct((s.outs, s.features), BF16),
            jax.ShapeDtypeStruct((1, 128), F32),
        ),
        in_specs=[anywhere] * 4,
        out_specs=(anywhere, anywhere),
        scratch_shapes=list(scratch.values()),
        compiler_params=pltpu.CompilerParams(
            collective_id=0, has_side_effects=True, vmem_limit_bytes=48 * 1024 * 1024
        ),
    )(padded, lab, qr, pos)
    return out_c, out_v[0, : s.rows]


def build(mesh, y, x):
    z = mesh.shape["dp"] // 2

    def run(embeddings, outcomes, seed_index):
        devices = mesh.shape["dp"] * mesh.shape["cent"]
        s = Sizes(
            z, y, x, embeddings.shape[0] // devices, embeddings.shape[1],
            seed_index.shape[0] // mesh.shape["cent"],
        )
        return jax.shard_map(
            functools.partial(per_device, s),
            mesh=mesh,
            in_specs=(P(("dp", "cent"), None), P(("dp", "cent")), P("cent")),
            out_specs=(P(("cent", "dp"), None), P(("dp", "cent"))),
            check_vma=False,
        )(embeddings, outcomes, seed_index)

    return run


def solution(mesh):
    return build(mesh, mesh.shape["cent"] // 4, 4)
```

```python
import functools

import jax
import jax.numpy as jnp
from jax import lax
from jax.experimental import pallas as pl
from jax.experimental.pallas import tpu as pltpu
from jax.sharding import PartitionSpec as P

INVERSE_TEMP = 8.0
PSEUDO_COUNT = 1.0
ABSENT = -1e30
MESH = pl.DeviceIdType.MESH
F32 = jnp.float32
BF16 = jnp.bfloat16


class Sizes:
    def __init__(self, z, y, x, rows, features, seeds):
        self.z, self.y, self.x = z, y, x
        self.rows = rows
        self.chip = 2 * rows
        self.features = features
        self.half = features // 2
        self.slab = features // z
        self.local = (z // 2) * self.chip
        self.group = y * x * self.chip
        self.width = x * self.chip
        self.span = -(-self.width // 128) * 128
        self.seeds = seeds
        self.outs = seeds // (2 * z)
        self.lanes = -(-self.local // 128) * 128


def scratch_of(s):
    dma = pltpu.SemaphoreType.DMA
    v = pltpu.VMEM
    return dict(
        qr=v((2, s.seeds), jnp.int32),
        pos=pltpu.SMEM((s.seeds,), jnp.int32),
        score=v((1, 128), F32),
        in_sem=dma((4,)),
        store_sem=dma((s.z + 1,)),
        mine=v((32, s.features), BF16),
        theirs=v((32, s.features), BF16),
        block=v((s.chip, s.features), BF16),
        rows=v((s.y, s.x, s.chip, s.features), BF16),
        cents=v((2, s.local, s.features), BF16),
        lab_x=v((2, s.x, 1, s.span), F32),
        lab_y=v((s.y, 1, s.span), F32),
        cnt_s=v((s.x, s.y, s.lanes), F32),
        cnt_x=v((s.x, s.y, s.lanes), F32),
        cnt_t=v((s.y, 1, s.lanes), F32),
        cnt_y=v((s.y, 1, s.lanes), F32),
        logits=v((s.y, s.local, s.width), F32),
        tops=v((s.y, 1, s.width), F32),
        probs=v((s.y, s.local, s.width), BF16),
        st_s=v((3, s.y, 1, s.span), F32),
        st_x=v((3, 2, s.x, s.y, 1, s.span), F32),
        st_t=v((3, s.y, 1, s.span), F32),
        st_y=v((3, s.y, s.y, 1, s.span), F32),
        st_f=v((3, s.y, 1, s.span), F32),
        mw_s=v((2, 8, s.lanes), F32),
        mw_r=v((2, s.z, 8, s.lanes), F32),
        num_s=v((2, s.z, s.local, s.slab), BF16),
        num_r=v((2, s.z, s.local, s.slab), BF16),
        table=v((2, s.y, s.x, s.local, s.slab), BF16),
        wide=v((2 * s.y * s.x * s.local, s.slab), F32),
        picked=v((s.outs, s.slab), F32),
        out_s=v((s.z, s.outs, s.slab), BF16),
        out_r=v((s.z, s.outs, s.slab), BF16),
        core_sem=dma((2,)),
        share_sem=dma((2, 2, s.y)),
        a1_sem=dma((2, 2, s.x)),
        a2_sem=dma((2, 2, s.y)),
        b1_sem=dma((2, 2, 2 * s.y)),
        b2_sem=dma((2, 2, 2 * s.y * s.x)),
        cent_sem=dma((2, s.z)),
        lab_sem=dma((2, 2 * s.x)),
        laby_sem=dma((2, s.y)),
        cnt_sem=dma((2, s.x)),
        cnty_sem=dma((2, s.y)),
        stx_sem=dma((3, 2, 2 * s.x)),
        sty_sem=dma((3, 2, s.y)),
        mw_sem=dma((2, 2, s.z)),
        num_sem=dma((2, 2, 3 * s.z)),
        new_sem=dma((2, 2 * s.z)),
        out_sem=dma((2, s.z)),
    )


def kernel(s, names, emb, lab, qr_in, pos_in, out_c, out_v, *scratch):
    ref = dict(zip(names, scratch))
    mine, theirs, qr, pos, lab_x = (ref[name] for name in ("mine", "theirs", "qr", "pos", "lab_x"))
    dp, cent = lax.axis_index("dp"), lax.axis_index("cent")
    z, core = dp // 2, dp % 2
    y, x = cent // s.x, cent % s.x

    def device(z_, core_, y_, x_):
        return (z_ * 2 + core_, y_ * s.x + x_)

    to_z = lambda p: device(p, core, y, x)
    to_y = lambda p: device(z, core, p, x)
    to_x = lambda p: device(z, core, y, p)
    to_cx = lambda p: device(z, p // s.x, y, p % s.x)
    partner = device(z, 1 - core, y, x)
    cx = core * s.x + x

    def each(n, me, do):
        def step(i, carry):
            do(lax.rem(me + i, n))
            return carry

        lax.fori_loop(1, n, step, 0)

    def copy(src, dst, sems, out_index, in_index, to):
        return pltpu.make_async_remote_copy(
            src_ref=src,
            dst_ref=dst,
            send_sem=sems.at[0, out_index],
            recv_sem=sems.at[1, in_index],
            device_id=to,
            device_id_type=MESH,
        )

    pending = []
    later = []

    class Exchange:
        def __init__(self, n, me, to, sems, src, dst):
            self.n, self.me, self.to, self.sems, self.src, self.dst = n, me, to, sems, src, dst

        def start(self):
            each(self.n, self.me, lambda p: copy(
                self.src(p), self.dst(self.me), self.sems, p, self.me, self.to(p)).start())
            pending.append(self)

        def arrived(self):
            each(self.n, self.me, lambda p: copy(
                self.src(p), self.dst(p), self.sems, p, p, self.to(p)).wait_recv())

        def sent(self):
            each(self.n, self.me, lambda p: copy(
                self.src(p), self.dst(self.me), self.sems, p, self.me, self.to(p)).wait_send())

    loads = [
        pltpu.make_async_copy(src, dst, ref["in_sem"].at[i])
        for i, (src, dst) in enumerate(((emb, mine), (lab, lab_x.at[core, x]), (qr_in, qr), (pos_in, pos)))
    ]
    for load in loads:
        load.start()
    barrier = pltpu.get_barrier_semaphore()

    def greet(to):
        return lambda p: pl.semaphore_signal(barrier, inc=1, device_id=to(p), device_id_type=MESH)

    each(2 * s.x, cx, greet(to_cx))
    each(s.y, y, greet(to_y))
    each(s.z, z, greet(to_z))
    pl.semaphore_wait(barrier, 2 * s.x - 1 + s.y - 1 + s.z - 1)

    loads[0].wait()
    swap = pltpu.make_async_remote_copy(
        src_ref=mine, dst_ref=theirs, send_sem=ref["core_sem"].at[0],
        recv_sem=ref["core_sem"].at[1], device_id=partner, device_id_type=MESH,
    )
    swap.start()

    swap.wait_recv()
    rows, block = ref["rows"], ref["block"]
    own = mine[...].astype(F32)[: s.rows]
    other = theirs[...].astype(F32)[: s.rows]
    first = jnp.where(core == 0, own, other)
    second = jnp.where(core == 0, other, own)
    block[...] = jnp.concatenate([first, second], axis=0).astype(BF16)

    def near_first(j):
        far = (j + 1) // 2
        return lax.rem(y + jnp.where(j % 2 == 1, far, s.y - far), s.y)

    class Plane:
        def __init__(self, t, at, row, use):
            self.at, self.row, self.use = at, row, use
            self.sems = {name: ref[name + "_sem"].at[t] for name in ("share", "a1", "a2", "b1", "b2")}

        def a1(self, p, source):
            piece = self.at(y, source, 0)
            return copy(piece, piece, self.sems["a1"], p, source, to_x(p))

        def a2(self, p, source):
            piece = self.at(source, everything, 0)
            return copy(piece, piece, self.sems["a2"], p, source, to_y(p))

        def b1(self, k, p, source):
            piece = self.at(source, x, k)
            first = (k - 1) * s.y
            return copy(piece, piece, self.sems["b1"], first + p, first + source, to_y(p))

        def b2(self, k, yy, p, source):
            piece = self.at(yy, source, k)
            first = ((k - 1) * s.y + yy) * s.x
            return copy(piece, piece, self.sems["b2"], first + p, first + source, to_x(p))

        def share(self, yy, side):
            piece = self.row(yy, side)
            return copy(piece, piece, self.sems["share"], yy, yy, partner)

        def along_y(self, do):
            def step(j, carry):
                do(near_first(j))
                return carry

            lax.fori_loop(1, s.y, step, 0)

        def start_a(self):
            each(s.x, x, lambda p: self.a1(p, x).start())

        def start_b(self, k):
            self.along_y(lambda p: self.b1(k, p, y).start())
            each(s.x, x, lambda p: self.b2(k, y, p, x).start())

        def sent(self):
            each(s.x, x, lambda p: self.a1(p, x).wait_send())
            self.along_y(lambda p: self.a2(p, y).wait_send())
            for k in (1, 2):
                self.along_y(lambda p: self.b1(k, p, y).wait_send())

            def step(yy, carry):
                for k in (1, 2):
                    each(s.x, x, lambda p: self.b2(k, yy, p, x).wait_send())
                self.share(yy, core).wait_send()
                return carry

            lax.fori_loop(0, s.y, step, 0)

        def spread(self, k, low, high):
            def step(j, carry):
                source = near_first(j)
                self.b1(k, source, source).wait_recv()
                each(s.x, x, lambda p: self.b2(k, source, p, x).start())
                return carry

            lax.fori_loop(low, high, step, 0)

        def turn(self):
            each(s.x, x, lambda p: self.a1(p, p).wait_recv())
            self.along_y(lambda p: self.a2(p, y).start())

        def finish(self):
            def step(j, carry):
                @pl.when(j < s.y)
                def _():
                    source = near_first(j)

                    @pl.when(j > 0)
                    def _():
                        self.a2(source, source).wait_recv()

                    for k in (1, 2):
                        each(s.x, x, lambda p: self.b2(k, source, p, p).wait_recv())
                    self.share(source, core).start()

                @pl.when(j > 0)
                def _():
                    source = near_first(j - 1)
                    self.share(source, 1 - core).wait_recv()
                    self.use(source)

                return carry

            lax.fori_loop(0, s.y + 1, step, 0)

    def lanes_of(c):
        return pl.ds(pl.multiple_of(c * s.half, 128), s.half)

    logits, probs, tops = ref["logits"], ref["probs"], ref["tops"]
    cents = ref["cents"]
    everything = slice(None)

    def rows_of(b, lanes):
        return rows[b, :, :, lanes].reshape(s.width, -1)

    def products_of(t):
        def use(b):
            logits[b] = lax.dot_general(
                cents[t], rows_of(b, everything), (((1,), (1,)), ((), ())), preferred_element_type=F32
            )

        return use

    rows[y, x, :, lanes_of(core)] = block[:, lanes_of(core)]
    quarter = s.half // 4
    row_parts = ((0, quarter), (quarter, s.half - 2 * quarter), (s.half - quarter, quarter))

    def rows_at(yy, xx, k):
        start, size = row_parts[k]
        return rows.at[yy, xx, :, pl.ds(pl.multiple_of(core * s.half + start, 128), size)]

    gather = Plane(0, rows_at, lambda yy, c: rows.at[yy, :, :, lanes_of(c)], products_of(0))
    pending.append(gather)
    gather.start_a()
    gather.start_b(1)
    gather.start_b(2)

    zh = s.z // 2

    def cent_copy(src_z, to):
        place = pl.ds(pl.multiple_of((src_z % zh) * s.chip, 16), s.chip)
        return copy(block, cents.at[0, place, :], ref["cent_sem"], to, src_z, to_z(to))

    @pl.when(z // zh == core)
    def _():
        each(s.z, z, lambda p: cent_copy(z, p).start())
        cents[0, pl.ds(pl.multiple_of((z % zh) * s.chip, 16), s.chip), :] = block[...]

    lab_ex = Exchange(2 * s.x, cx, to_cx, ref["lab_sem"],
                      lambda p: lab_x.at[core, x], lambda p: lab_x.at[p // s.x, p % s.x])
    loads[1].wait()
    lab_ex.start()
    loads[2].wait()
    loads[3].wait()

    cnt_s, cnt_x = ref["cnt_s"], ref["cnt_x"]
    places = lax.broadcasted_iota(jnp.int32, (s.lanes, s.seeds), 0)
    hot_r = jnp.where(places == qr[1:2, :], 1.0, 0.0).astype(BF16)
    for xx in range(s.x):
        owner = lax.broadcasted_iota(jnp.int32, (s.y, s.seeds), 0) * s.x + (xx + core * s.x * s.y)
        hot_q = jnp.where(owner == qr[0:1, :], 1.0, 0.0).astype(BF16)
        cnt_s[xx] = lax.dot_general(hot_q, hot_r, (((1,), (1,)), ((), ())), preferred_element_type=F32)
    cnt_ex = Exchange(s.x, x, to_x, ref["cnt_sem"], lambda p: cnt_s.at[p], lambda p: cnt_x.at[p])
    cnt_ex.start()
    gather.spread(1, 1, s.y)
    gather.turn()

    cnt_ex.arrived()
    cnt_x[x] = cnt_s[x]
    total = cnt_x[0]
    for xx in range(1, s.x):
        total = total + cnt_x[xx]
    cnt_t, cnt_y = ref["cnt_t"], ref["cnt_y"]
    for yy in range(s.y):
        cnt_t[yy] = total[yy : yy + 1]
    cnty_ex = Exchange(s.y, y, to_y, ref["cnty_sem"], lambda p: cnt_t.at[p], lambda p: cnt_y.at[p])
    cnty_ex.start()
    lab_ex.arrived()
    lab_y = ref["lab_y"]
    line = lab_x[0, 0]
    for i in range(1, 2 * s.x):
        line = line + lab_x[i // s.x, i % s.x]
    lab_y[y] = line
    laby_ex = Exchange(s.y, y, to_y, ref["laby_sem"], lambda p: lab_y.at[y], lambda p: lab_y.at[p])
    laby_ex.start()

    def cents_in(i, carry):
        src_z = core * zh + i

        @pl.when(src_z != z)
        def _():
            place = pl.ds(pl.multiple_of(i * s.chip, 16), s.chip)
            copy(block, cents.at[0, place, :], ref["cent_sem"], src_z, src_z, to_z(src_z)).wait_recv()

        return carry

    gather.spread(2, 1, s.y)
    lax.fori_loop(0, zh, cents_in, 0)
    gather.finish()

    def to_column(row):
        eye = lax.broadcasted_iota(jnp.int32, (s.local, s.lanes), 0) == lax.broadcasted_iota(
            jnp.int32, (s.local, s.lanes), 1
        )
        return jnp.sum(jnp.where(eye, row, 0.0), axis=1, keepdims=True)

    cnty_ex.arrived()
    cnt_y[y] = cnt_t[y]
    line = cnt_y[0]
    for yy in range(1, s.y):
        line = line + cnt_y[yy]
    weight = to_column(line)
    laby_ex.arrived()

    ref["st_s"][...] = jnp.zeros_like(ref["st_s"])

    def blocks(do):
        def step(b, carry):
            do(2 * b)
            do(2 * b + 1)
            return carry

        lax.fori_loop(0, s.y // 2, step, 0)

    def lse_of(parts):
        top = functools.reduce(jnp.maximum, parts)
        return top + jnp.log(sum(jnp.exp(part - top) for part in parts))

    def total_of(parts):
        return sum(parts)

    def all_reduce(t, combine):
        st_s, st_x, st_t, st_y = (ref[name].at[t] for name in ("st_s", "st_x", "st_t", "st_y"))
        near = Exchange(2 * s.x, cx, to_cx, ref["stx_sem"].at[t], lambda p: st_s, lambda p: st_x.at[p // s.x, p % s.x])
        far = Exchange(s.y, y, to_y, ref["sty_sem"].at[t], lambda p: st_t, lambda p: st_y.at[p])
        near.start()
        yield
        near.arrived()
        st_x[core, x] = st_s[...]
        st_t[...] = combine([st_x[i // s.x, i % s.x] for i in range(2 * s.x)])
        far.start()
        yield
        far.arrived()
        st_y[y] = st_t[...]
        ref["st_f"][t] = combine([st_y[i] for i in range(s.y)])

    table, wide = ref["table"], ref["wide"]

    def widen(yy):
        size = s.x * s.local
        for a in range(2):
            wide[pl.ds(pl.multiple_of((a * s.y + yy) * size, 16), size), :] = (
                table[a, yy].reshape(size, s.slab).astype(F32)
            )

    low = 48
    rest = (s.local - low) // 32 * 16
    new_parts = ((0, rest), (rest, s.local - low - rest), (s.local - low, low))

    def table_at(yy, xx, k):
        start, size = new_parts[(k + 2) % 3]
        return table.at[core, yy, xx, pl.ds(start, size), :]

    gather = Plane(1, table_at, lambda yy, c: table.at[c, yy], widen)
    pending.append(gather)

    for t in range(2):
        held = cents.at[t]
        exact = held[...].astype(F32)
        norm = jnp.sum(exact * exact, axis=1, keepdims=True)
        bias = jnp.where(weight > 0.0, (-0.5 * INVERSE_TEMP) * norm, ABSENT)
        st_s = ref["st_s"].at[t]

        if t == 1:
            blocks(products_of(1))

        def scores_of(b):
            value = jnp.where(weight > 0.0, INVERSE_TEMP * logits[b] + bias, ABSENT)
            top = jnp.max(value, axis=0, keepdims=True)
            power = jnp.exp(value - top)
            logits[b] = power
            tops[b] = top
            mass = jnp.sum(weight * power, axis=0, keepdims=True)
            st_s[b, :, : s.width] = jnp.maximum(top + jnp.log(mass), ABSENT)

        blocks(scores_of)
        for _ in all_reduce(t, lse_of):
            pass
        norm_of = ref["st_f"].at[t]
        mw_s, mw_r = ref["mw_s"].at[t], ref["mw_r"].at[t]
        mw_s[...] = jnp.zeros_like(mw_s)

        def shares_of(b):
            value = logits[b] * jnp.exp(tops[b] - norm_of[b, :, : s.width])
            if t == 1:
                logits[b] = value
            rounded = value.astype(BF16)
            probs[b] = rounded
            label = lab_y[b, :, : s.width]
            line = lax.broadcasted_iota(jnp.int32, (8, s.width), 0)
            left = jnp.where(line == 0, 1.0, jnp.where(line == 1, label, 0.0)).astype(BF16)
            both = lax.dot_general(left, rounded, (((1,), (1,)), ((), ())), preferred_element_type=F32)
            mw_s[:, : s.local] += both

        blocks(shares_of)
        mw_ex = Exchange(s.z, z, to_z, ref["mw_sem"].at[t], lambda p: mw_s, lambda p: mw_r.at[p])
        mw_ex.start()

        num_s, num_r = ref["num_s"].at[t], ref["num_r"].at[t]
        half = s.local // 2
        parts = ((0, half), (half, half)) if t == 0 else new_parts

        def num_copy(k, p, source, t=t, parts=parts, num_s=num_s, num_r=num_r):
            piece = pl.ds(parts[k][0], parts[k][1])
            return copy(num_s.at[p, piece, :], num_r.at[source, piece, :], ref["num_sem"].at[t],
                        k * s.z + p, k * s.z + source, to_z(p))

        pairs = s.z // 2

        def numer_of(i, carry):
            pair = lax.rem(z // 2 + 1 + i, pairs)
            lanes = pl.ds(pl.multiple_of(pair * 2 * s.slab, 128), 2 * s.slab)
            acc = jnp.zeros((s.local, 2 * s.slab), F32)
            for b in range(s.y):
                acc = acc + jnp.dot(probs[b], rows_of(b, lanes), preferred_element_type=F32)
            for side in range(2):
                p = pair * 2 + side
                num_s[p] = acc[:, side * s.slab : (side + 1) * s.slab].astype(BF16)

                @pl.when(p != z)
                def _():
                    num_copy(0, p, z).start()

            return carry

        lax.fori_loop(0, pairs, numer_of, 0)
        for k in range(1, len(parts)):
            each(s.z, z, lambda p: num_copy(k, p, z).start())
        mw_ex.arrived()
        mw_r[z] = mw_s[...]
        both = mw_r[0]
        for i in range(1, s.z):
            both = both + mw_r[i]
        mass = to_column(both[0:1])
        if t == 1:
            wins = to_column(both[1:2])
            rate = weight * ((wins + 0.5 * PSEUDO_COUNT) / (mass + PSEUDO_COUNT))
            sc = ref["st_s"].at[2]

            def step_scores(b):
                sc[b, :, : s.width] = jnp.sum(logits[b] * rate, axis=0, keepdims=True)

            blocks(step_scores)
            reduce_scores = all_reduce(2, total_of)
            next(reduce_scores)
        mylanes = pl.ds(pl.multiple_of(z * s.slab, 128), s.slab)

        def fresh(k):
            each(s.z, z, lambda p: num_copy(k, p, p).wait_recv())
            first, size = parts[k]
            piece = slice(first, first + size)
            num_r[z, piece, :] = num_s[z, piece, :]
            acc = num_r[0, piece, :].astype(F32)
            for i in range(1, s.z):
                acc = acc + num_r[i, piece, :].astype(F32)
            acc = acc + PSEUDO_COUNT * held[piece, mylanes].astype(F32)
            return (acc / (mass[piece] + PSEUDO_COUNT)).astype(BF16)

        if t == 0:
            def new_copy(k, p, source, parts=parts):
                lanes = pl.ds(pl.multiple_of(source * s.slab, 128), s.slab)
                piece = cents.at[1, pl.ds(parts[k][0], parts[k][1]), lanes]
                return copy(piece, piece, ref["new_sem"], k * s.z + p, k * s.z + source, to_z(p))

            for k in range(2):
                cents[1, parts[k][0] : parts[k][0] + parts[k][1], mylanes] = fresh(k)
                each(s.z, z, lambda p: new_copy(k, p, z).start())
            for k in range(2):
                each(s.z, z, lambda p: new_copy(k, p, p).wait_recv())
        else:
            for k in range(3):
                table[core, y, x, parts[k][0] : parts[k][0] + parts[k][1], :] = fresh(k)
                if k < 2:
                    gather.start_b(k + 1)
                else:
                    gather.start_a()
        later.append((num_copy, len(parts)))
        if t == 0:
            later.append((new_copy, 2))

    next(reduce_scores)
    gather.spread(1, 1, s.y)
    gather.turn()
    gather.spread(2, 1, s.y)
    for _ in reduce_scores:
        pass
    final = ref["st_f"]
    offset = x * s.chip + core * s.rows
    n_out = 32
    here = lax.broadcasted_iota(jnp.int32, (n_out, s.span), 1)
    wanted = lax.broadcasted_iota(jnp.int32, (n_out, s.span), 0) + offset
    column = jnp.sum(jnp.where(here == wanted, final[2, y], 0.0), axis=1, keepdims=True)
    eye = lax.broadcasted_iota(jnp.int32, (n_out, 128), 0) == lax.broadcasted_iota(jnp.int32, (n_out, 128), 1)
    ref["score"][...] = jnp.sum(jnp.where(eye, column, 0.0), axis=0, keepdims=True)
    store_score = pltpu.make_async_copy(ref["score"], out_v, ref["store_sem"].at[s.z])
    store_score.start()
    gather.finish()
    picked, out_s, out_r = ref["picked"], ref["out_s"], ref["out_r"]
    out_ex = Exchange(s.z, z, to_z, ref["out_sem"], lambda p: out_s.at[p], lambda p: out_r.at[p])

    def pick(i, carry):
        p = lax.rem(z + 1 + i, s.z)
        base = (2 * p + core) * s.outs

        def eight(j, carry):
            for k in range(8):
                n = j * 8 + k
                picked[pl.ds(n, 1), :] = wide[pl.ds(pos[base + n], 1), :]
            return carry

        lax.fori_loop(0, s.outs // 8, eight, 0)
        out_s[p] = picked[...].astype(BF16)

        @pl.when(p != z)
        def _():
            copy(out_s.at[p], out_r.at[z], ref["out_sem"], p, z, to_z(p)).start()

        return carry

    lax.fori_loop(0, s.z, pick, 0)
    swap.wait_send()

    @pl.when(z // zh == core)
    def _():
        each(s.z, z, lambda p: cent_copy(z, p).wait_send())

    for exchange in pending:
        exchange.sent()
    for sent_copy, count in later:
        for k in range(count):
            each(s.z, z, lambda p: sent_copy(k, p, z).wait_send())
    def store(p, block):
        lanes = pl.ds(pl.multiple_of(p * s.slab, 128), s.slab)
        return pltpu.make_async_copy(block, out_c.at[:, lanes], ref["store_sem"].at[p])

    store(z, out_s.at[z]).start()

    def keep(i, carry):
        p = lax.rem(z + s.z - i, s.z)
        copy(out_s.at[p], out_r.at[p], ref["out_sem"], p, p, to_z(p)).wait_recv()
        store(p, out_r.at[p]).start()
        return carry

    lax.fori_loop(1, s.z, keep, 0)
    out_ex.sent()
    store_score.wait()
    store(z, out_s.at[z]).wait()
    each(s.z, z, lambda p: store(p, out_r.at[p]).wait())


def per_device(s, embeddings, outcomes, seed_index):
    core = lax.axis_index("dp") % 2
    cent = lax.axis_index("cent")
    plane = s.rows * s.x * s.y
    dp, rest = seed_index // plane, seed_index % plane
    zs, side = dp // 2, dp % 2
    zh = s.z // 2
    q = (zs // zh) * (s.x * s.y) + rest // s.rows
    r = (zs % zh) * s.chip + side * s.rows + rest % s.rows
    qr = jnp.stack([q, r])
    pos = q * s.local + r
    offset = (cent % s.x) * s.chip + core * s.rows
    spot = lax.broadcasted_iota(jnp.int32, (s.rows, s.span), 1) - lax.broadcasted_iota(
        jnp.int32, (s.rows, s.span), 0
    )
    lab = jnp.sum(
        jnp.where(spot == offset, outcomes.astype(F32)[:, None], 0.0), axis=0, keepdims=True
    )
    scratch = scratch_of(s)
    anywhere = pl.BlockSpec(memory_space=pl.ANY)
    padded = jnp.pad(embeddings, ((0, 32 - s.rows), (0, 0)))
    out_c, out_v = pl.pallas_call(
        functools.partial(kernel, s, tuple(scratch)),
        out_shape=(
            jax.ShapeDtypeStruct((s.outs, s.features), BF16),
            jax.ShapeDtypeStruct((1, 128), F32),
        ),
        in_specs=[anywhere] * 4,
        out_specs=(anywhere, anywhere),
        scratch_shapes=list(scratch.values()),
        compiler_params=pltpu.CompilerParams(
            collective_id=0, has_side_effects=True, vmem_limit_bytes=48 * 1024 * 1024
        ),
    )(padded, lab, qr, pos)
    return out_c, out_v[0, : s.rows]


def build(mesh, y, x):
    z = mesh.shape["dp"] // 2

    def run(embeddings, outcomes, seed_index):
        devices = mesh.shape["dp"] * mesh.shape["cent"]
        s = Sizes(
            z, y, x, embeddings.shape[0] // devices, embeddings.shape[1],
            seed_index.shape[0] // mesh.shape["cent"],
        )
        return jax.shard_map(
            functools.partial(per_device, s),
            mesh=mesh,
            in_specs=(P(("dp", "cent"), None), P(("dp", "cent")), P("cent")),
            out_specs=(P(("cent", "dp"), None), P(("dp", "cent"))),
            check_vma=False,
        )(embeddings, outcomes, seed_index)

    return run


def solution(mesh):
    return build(mesh, mesh.shape["cent"] // 4, 4)
```

```python
import functools

import jax
import jax.numpy as jnp
from jax import lax
from jax.experimental import pallas as pl
from jax.experimental.pallas import tpu as pltpu
from jax.sharding import PartitionSpec as P

INVERSE_TEMP = 8.0
PSEUDO_COUNT = 1.0
ABSENT = -1e30
MESH = pl.DeviceIdType.MESH
F32 = jnp.float32
BF16 = jnp.bfloat16


class Sizes:
    def __init__(self, z, y, x, rows, features, seeds):
        self.z, self.y, self.x = z, y, x
        self.rows = rows
        self.chip = 2 * rows
        self.features = features
        self.half = features // 2
        self.slab = features // z
        self.local = (z // 2) * self.chip
        self.group = y * x * self.chip
        self.width = x * self.chip
        self.span = -(-self.width // 128) * 128
        self.seeds = seeds
        self.outs = seeds // (2 * z)
        self.lanes = -(-self.local // 128) * 128


def scratch_of(s):
    dma = pltpu.SemaphoreType.DMA
    v = pltpu.VMEM
    return dict(
        qr=v((2, s.seeds), jnp.int32),
        pos=pltpu.SMEM((s.seeds,), jnp.int32),
        score=v((1, 128), F32),
        in_sem=dma((4,)),
        store_sem=dma((s.z + 1,)),
        mine=v((32, s.features), BF16),
        theirs=v((32, s.features), BF16),
        block=v((s.chip, s.features), BF16),
        rows=v((s.y, s.x, s.chip, s.features), BF16),
        cents=v((2, s.local, s.features), BF16),
        lab_x=v((2, s.x, 1, s.span), F32),
        lab_y=v((s.y, 1, s.span), F32),
        cnt_s=v((s.x, s.y, s.lanes), F32),
        cnt_x=v((s.x, s.y, s.lanes), F32),
        cnt_t=v((s.y, 1, s.lanes), F32),
        cnt_y=v((s.y, 1, s.lanes), F32),
        logits=v((s.y, s.local, s.width), F32),
        tops=v((s.y, 1, s.width), F32),
        probs=v((s.y, s.local, s.width), BF16),
        st_s=v((3, s.y, 1, s.span), F32),
        st_x=v((3, 2, s.x, s.y, 1, s.span), F32),
        st_t=v((3, s.y, 1, s.span), F32),
        st_y=v((3, s.y, s.y, 1, s.span), F32),
        st_f=v((3, s.y, 1, s.span), F32),
        mw_s=v((2, 8, s.lanes), F32),
        mw_r=v((2, s.z, 8, s.lanes), F32),
        num_s=v((2, s.z, s.local, s.slab), BF16),
        num_r=v((2, s.z, s.local, s.slab), BF16),
        table=v((2, s.y, s.x, s.local, s.slab), BF16),
        wide=v((2 * s.y * s.x * s.local, s.slab), F32),
        picked=v((s.outs, s.slab), F32),
        out_s=v((s.z, s.outs, s.slab), BF16),
        out_r=v((s.z, s.outs, s.slab), BF16),
        core_sem=dma((2,)),
        share_sem=dma((2, 2, s.y)),
        a1_sem=dma((2, 2, s.x)),
        a2_sem=dma((2, 2, s.y)),
        b1_sem=dma((2, 2, 2 * s.y)),
        b2_sem=dma((2, 2, 2 * s.y * s.x)),
        cent_sem=dma((2, s.z)),
        lab_sem=dma((2, 2 * s.x)),
        laby_sem=dma((2, s.y)),
        cnt_sem=dma((2, s.x)),
        cnty_sem=dma((2, s.y)),
        stx_sem=dma((3, 2, 2 * s.x)),
        sty_sem=dma((3, 2, s.y)),
        mw_sem=dma((2, 2, s.z)),
        num_sem=dma((2, 2, 3 * s.z)),
        new_sem=dma((2, 2 * s.z)),
        out_sem=dma((2, s.z)),
    )


def kernel(s, names, emb, lab, qr_in, pos_in, out_c, out_v, *scratch):
    ref = dict(zip(names, scratch))
    mine, theirs, qr, pos, lab_x = (ref[name] for name in ("mine", "theirs", "qr", "pos", "lab_x"))
    dp, cent = lax.axis_index("dp"), lax.axis_index("cent")
    z, core = dp // 2, dp % 2
    y, x = cent // s.x, cent % s.x

    def device(z_, core_, y_, x_):
        return (z_ * 2 + core_, y_ * s.x + x_)

    to_z = lambda p: device(p, core, y, x)
    to_y = lambda p: device(z, core, p, x)
    to_x = lambda p: device(z, core, y, p)
    to_cx = lambda p: device(z, p // s.x, y, p % s.x)
    partner = device(z, 1 - core, y, x)
    cx = core * s.x + x

    def each(n, me, do):
        def step(i, carry):
            do(lax.rem(me + i, n))
            return carry

        lax.fori_loop(1, n, step, 0)

    def copy(src, dst, sems, out_index, in_index, to):
        return pltpu.make_async_remote_copy(
            src_ref=src,
            dst_ref=dst,
            send_sem=sems.at[0, out_index],
            recv_sem=sems.at[1, in_index],
            device_id=to,
            device_id_type=MESH,
        )

    pending = []
    later = []

    class Exchange:
        def __init__(self, n, me, to, sems, src, dst):
            self.n, self.me, self.to, self.sems, self.src, self.dst = n, me, to, sems, src, dst

        def start(self):
            each(self.n, self.me, lambda p: copy(
                self.src(p), self.dst(self.me), self.sems, p, self.me, self.to(p)).start())
            pending.append(self)

        def arrived(self):
            each(self.n, self.me, lambda p: copy(
                self.src(p), self.dst(p), self.sems, p, p, self.to(p)).wait_recv())

        def sent(self):
            each(self.n, self.me, lambda p: copy(
                self.src(p), self.dst(self.me), self.sems, p, self.me, self.to(p)).wait_send())

    loads = [
        pltpu.make_async_copy(src, dst, ref["in_sem"].at[i])
        for i, (src, dst) in enumerate(((emb, mine), (lab, lab_x.at[core, x]), (qr_in, qr), (pos_in, pos)))
    ]
    for load in loads:
        load.start()
    barrier = pltpu.get_barrier_semaphore()

    def greet(to):
        return lambda p: pl.semaphore_signal(barrier, inc=1, device_id=to(p), device_id_type=MESH)

    each(2 * s.x, cx, greet(to_cx))
    each(s.y, y, greet(to_y))
    each(s.z, z, greet(to_z))
    pl.semaphore_wait(barrier, 2 * s.x - 1 + s.y - 1 + s.z - 1)

    loads[0].wait()
    swap = pltpu.make_async_remote_copy(
        src_ref=mine, dst_ref=theirs, send_sem=ref["core_sem"].at[0],
        recv_sem=ref["core_sem"].at[1], device_id=partner, device_id_type=MESH,
    )
    swap.start()

    swap.wait_recv()
    rows, block = ref["rows"], ref["block"]
    own = mine[...].astype(F32)[: s.rows]
    other = theirs[...].astype(F32)[: s.rows]
    first = jnp.where(core == 0, own, other)
    second = jnp.where(core == 0, other, own)
    block[...] = jnp.concatenate([first, second], axis=0).astype(BF16)

    def near_first(j):
        far = (j + 1) // 2
        return lax.rem(y + jnp.where(j % 2 == 1, far, s.y - far), s.y)

    class Plane:
        def __init__(self, t, at, row, use):
            self.at, self.row, self.use = at, row, use
            self.sems = {name: ref[name + "_sem"].at[t] for name in ("share", "a1", "a2", "b1", "b2")}

        def a1(self, p, source):
            piece = self.at(y, source, 0)
            return copy(piece, piece, self.sems["a1"], p, source, to_x(p))

        def a2(self, p, source):
            piece = self.at(source, everything, 0)
            return copy(piece, piece, self.sems["a2"], p, source, to_y(p))

        def b1(self, k, p, source):
            piece = self.at(source, x, k)
            first = (k - 1) * s.y
            return copy(piece, piece, self.sems["b1"], first + p, first + source, to_y(p))

        def b2(self, k, yy, p, source):
            piece = self.at(yy, source, k)
            first = ((k - 1) * s.y + yy) * s.x
            return copy(piece, piece, self.sems["b2"], first + p, first + source, to_x(p))

        def share(self, yy, side):
            piece = self.row(yy, side)
            return copy(piece, piece, self.sems["share"], yy, yy, partner)

        def along_y(self, do):
            def step(j, carry):
                do(near_first(j))
                return carry

            lax.fori_loop(1, s.y, step, 0)

        def start_a(self):
            each(s.x, x, lambda p: self.a1(p, x).start())

        def start_b(self, k):
            self.along_y(lambda p: self.b1(k, p, y).start())
            each(s.x, x, lambda p: self.b2(k, y, p, x).start())

        def sent(self):
            each(s.x, x, lambda p: self.a1(p, x).wait_send())
            self.along_y(lambda p: self.a2(p, y).wait_send())
            for k in (1, 2):
                self.along_y(lambda p: self.b1(k, p, y).wait_send())

            def step(yy, carry):
                for k in (1, 2):
                    each(s.x, x, lambda p: self.b2(k, yy, p, x).wait_send())
                self.share(yy, core).wait_send()
                return carry

            lax.fori_loop(0, s.y, step, 0)

        def spread(self, k, low, high):
            def step(j, carry):
                source = near_first(j)
                self.b1(k, source, source).wait_recv()
                each(s.x, x, lambda p: self.b2(k, source, p, x).start())
                return carry

            lax.fori_loop(low, high, step, 0)

        def turn(self):
            each(s.x, x, lambda p: self.a1(p, p).wait_recv())
            self.along_y(lambda p: self.a2(p, y).start())

        def finish(self):
            def step(j, carry):
                @pl.when(j < s.y)
                def _():
                    source = near_first(j)

                    @pl.when(j > 0)
                    def _():
                        self.a2(source, source).wait_recv()

                    for k in (1, 2):
                        each(s.x, x, lambda p: self.b2(k, source, p, p).wait_recv())
                    self.share(source, core).start()

                @pl.when(j > 0)
                def _():
                    source = near_first(j - 1)
                    self.share(source, 1 - core).wait_recv()
                    self.use(source)

                return carry

            lax.fori_loop(0, s.y + 1, step, 0)

    def lanes_of(c):
        return pl.ds(pl.multiple_of(c * s.half, 128), s.half)

    logits, probs, tops = ref["logits"], ref["probs"], ref["tops"]
    cents = ref["cents"]
    everything = slice(None)

    def rows_of(b, lanes):
        return rows[b, :, :, lanes].reshape(s.width, -1)

    def products_of(t):
        def use(b):
            logits[b] = lax.dot_general(
                cents[t], rows_of(b, everything), (((1,), (1,)), ((), ())), preferred_element_type=F32
            )

        return use

    rows[y, x, :, lanes_of(core)] = block[:, lanes_of(core)]
    quarter = s.half // 4
    row_parts = ((0, quarter), (quarter, s.half - 2 * quarter), (s.half - quarter, quarter))

    def rows_at(yy, xx, k):
        start, size = row_parts[k]
        return rows.at[yy, xx, :, pl.ds(pl.multiple_of(core * s.half + start, 128), size)]

    gather = Plane(0, rows_at, lambda yy, c: rows.at[yy, :, :, lanes_of(c)], products_of(0))
    pending.append(gather)
    gather.start_a()
    gather.start_b(1)
    gather.start_b(2)

    zh = s.z // 2

    def cent_copy(src_z, to):
        place = pl.ds(pl.multiple_of((src_z % zh) * s.chip, 16), s.chip)
        return copy(block, cents.at[0, place, :], ref["cent_sem"], to, src_z, to_z(to))

    @pl.when(z // zh == core)
    def _():
        each(s.z, z, lambda p: cent_copy(z, p).start())
        cents[0, pl.ds(pl.multiple_of((z % zh) * s.chip, 16), s.chip), :] = block[...]

    lab_ex = Exchange(2 * s.x, cx, to_cx, ref["lab_sem"],
                      lambda p: lab_x.at[core, x], lambda p: lab_x.at[p // s.x, p % s.x])
    loads[1].wait()
    lab_ex.start()
    loads[2].wait()
    loads[3].wait()

    cnt_s, cnt_x = ref["cnt_s"], ref["cnt_x"]
    places = lax.broadcasted_iota(jnp.int32, (s.lanes, s.seeds), 0)
    hot_r = jnp.where(places == qr[1:2, :], 1.0, 0.0).astype(BF16)
    for xx in range(s.x):
        owner = lax.broadcasted_iota(jnp.int32, (s.y, s.seeds), 0) * s.x + (xx + core * s.x * s.y)
        hot_q = jnp.where(owner == qr[0:1, :], 1.0, 0.0).astype(BF16)
        cnt_s[xx] = lax.dot_general(hot_q, hot_r, (((1,), (1,)), ((), ())), preferred_element_type=F32)
    cnt_ex = Exchange(s.x, x, to_x, ref["cnt_sem"], lambda p: cnt_s.at[p], lambda p: cnt_x.at[p])
    cnt_ex.start()
    gather.spread(1, 1, s.y)
    gather.turn()

    cnt_ex.arrived()
    cnt_x[x] = cnt_s[x]
    total = cnt_x[0]
    for xx in range(1, s.x):
        total = total + cnt_x[xx]
    cnt_t, cnt_y = ref["cnt_t"], ref["cnt_y"]
    for yy in range(s.y):
        cnt_t[yy] = total[yy : yy + 1]
    cnty_ex = Exchange(s.y, y, to_y, ref["cnty_sem"], lambda p: cnt_t.at[p], lambda p: cnt_y.at[p])
    cnty_ex.start()
    lab_ex.arrived()
    lab_y = ref["lab_y"]
    line = lab_x[0, 0]
    for i in range(1, 2 * s.x):
        line = line + lab_x[i // s.x, i % s.x]
    lab_y[y] = line
    laby_ex = Exchange(s.y, y, to_y, ref["laby_sem"], lambda p: lab_y.at[y], lambda p: lab_y.at[p])
    laby_ex.start()

    def cents_in(i, carry):
        src_z = core * zh + i

        @pl.when(src_z != z)
        def _():
            place = pl.ds(pl.multiple_of(i * s.chip, 16), s.chip)
            copy(block, cents.at[0, place, :], ref["cent_sem"], src_z, src_z, to_z(src_z)).wait_recv()

        return carry

    gather.spread(2, 1, s.y)
    lax.fori_loop(0, zh, cents_in, 0)
    gather.finish()

    def to_column(row):
        eye = lax.broadcasted_iota(jnp.int32, (s.local, s.lanes), 0) == lax.broadcasted_iota(
            jnp.int32, (s.local, s.lanes), 1
        )
        return jnp.sum(jnp.where(eye, row, 0.0), axis=1, keepdims=True)

    cnty_ex.arrived()
    cnt_y[y] = cnt_t[y]
    line = cnt_y[0]
    for yy in range(1, s.y):
        line = line + cnt_y[yy]
    weight = to_column(line)
    laby_ex.arrived()

    ref["st_s"][...] = jnp.zeros_like(ref["st_s"])

    def blocks(do):
        def step(b, carry):
            for i in range(4):
                do(4 * b + i)
            return carry

        lax.fori_loop(0, s.y // 4, step, 0)

    def lse_of(parts):
        top = functools.reduce(jnp.maximum, parts)
        return top + jnp.log(sum(jnp.exp(part - top) for part in parts))

    def total_of(parts):
        return sum(parts)

    def all_reduce(t, combine):
        st_s, st_x, st_t, st_y = (ref[name].at[t] for name in ("st_s", "st_x", "st_t", "st_y"))
        near = Exchange(2 * s.x, cx, to_cx, ref["stx_sem"].at[t], lambda p: st_s, lambda p: st_x.at[p // s.x, p % s.x])
        far = Exchange(s.y, y, to_y, ref["sty_sem"].at[t], lambda p: st_t, lambda p: st_y.at[p])
        near.start()
        yield
        near.arrived()
        st_x[core, x] = st_s[...]
        st_t[...] = combine([st_x[i // s.x, i % s.x] for i in range(2 * s.x)])
        far.start()
        yield
        far.arrived()
        st_y[y] = st_t[...]
        ref["st_f"][t] = combine([st_y[i] for i in range(s.y)])

    table, wide = ref["table"], ref["wide"]

    def widen(yy):
        size = s.x * s.local
        for a in range(2):
            wide[pl.ds(pl.multiple_of((a * s.y + yy) * size, 16), size), :] = (
                table[a, yy].reshape(size, s.slab).astype(F32)
            )

    low = 48
    rest = (s.local - low) // 32 * 16
    new_parts = ((0, rest), (rest, s.local - low - rest), (s.local - low, low))

    def table_at(yy, xx, k):
        start, size = new_parts[(k + 2) % 3]
        return table.at[core, yy, xx, pl.ds(start, size), :]

    gather = Plane(1, table_at, lambda yy, c: table.at[c, yy], widen)
    pending.append(gather)

    for t in range(2):
        held = cents.at[t]
        exact = held[...].astype(F32)
        norm = jnp.sum(exact * exact, axis=1, keepdims=True)
        bias = jnp.where(weight > 0.0, (-0.5 * INVERSE_TEMP) * norm, ABSENT)
        st_s = ref["st_s"].at[t]

        if t == 1:
            blocks(products_of(1))

        def scores_of(b):
            value = jnp.where(weight > 0.0, INVERSE_TEMP * logits[b] + bias, ABSENT)
            top = jnp.max(value, axis=0, keepdims=True)
            power = jnp.exp(value - top)
            logits[b] = power
            tops[b] = top
            mass = jnp.sum(weight * power, axis=0, keepdims=True)
            st_s[b, :, : s.width] = jnp.maximum(top + jnp.log(mass), ABSENT)

        blocks(scores_of)
        for _ in all_reduce(t, lse_of):
            pass
        norm_of = ref["st_f"].at[t]
        mw_s, mw_r = ref["mw_s"].at[t], ref["mw_r"].at[t]
        mw_s[...] = jnp.zeros_like(mw_s)

        def shares_of(b):
            value = logits[b] * jnp.exp(tops[b] - norm_of[b, :, : s.width])
            if t == 1:
                logits[b] = value
            rounded = value.astype(BF16)
            probs[b] = rounded
            label = lab_y[b, :, : s.width]
            line = lax.broadcasted_iota(jnp.int32, (8, s.width), 0)
            left = jnp.where(line == 0, 1.0, jnp.where(line == 1, label, 0.0)).astype(BF16)
            both = lax.dot_general(left, rounded, (((1,), (1,)), ((), ())), preferred_element_type=F32)
            mw_s[:, : s.local] += both

        blocks(shares_of)
        mw_ex = Exchange(s.z, z, to_z, ref["mw_sem"].at[t], lambda p: mw_s, lambda p: mw_r.at[p])
        mw_ex.start()

        num_s, num_r = ref["num_s"].at[t], ref["num_r"].at[t]
        half = s.local // 2
        parts = ((0, half), (half, half)) if t == 0 else new_parts

        def num_copy(k, p, source, t=t, parts=parts, num_s=num_s, num_r=num_r):
            piece = pl.ds(parts[k][0], parts[k][1])
            return copy(num_s.at[p, piece, :], num_r.at[source, piece, :], ref["num_sem"].at[t],
                        k * s.z + p, k * s.z + source, to_z(p))

        pairs = s.z // 2

        def numer_of(i, carry):
            pair = lax.rem(z // 2 + 1 + i, pairs)
            lanes = pl.ds(pl.multiple_of(pair * 2 * s.slab, 128), 2 * s.slab)
            acc = jnp.zeros((s.local, 2 * s.slab), F32)
            for b in range(s.y):
                acc = acc + jnp.dot(probs[b], rows_of(b, lanes), preferred_element_type=F32)
            for side in range(2):
                p = pair * 2 + side
                num_s[p] = acc[:, side * s.slab : (side + 1) * s.slab].astype(BF16)

                @pl.when(p != z)
                def _():
                    num_copy(0, p, z).start()

            return carry

        lax.fori_loop(0, pairs, numer_of, 0)
        for k in range(1, len(parts)):
            each(s.z, z, lambda p: num_copy(k, p, z).start())
        mw_ex.arrived()
        mw_r[z] = mw_s[...]
        both = mw_r[0]
        for i in range(1, s.z):
            both = both + mw_r[i]
        mass = to_column(both[0:1])
        if t == 1:
            wins = to_column(both[1:2])
            rate = weight * ((wins + 0.5 * PSEUDO_COUNT) / (mass + PSEUDO_COUNT))
            sc = ref["st_s"].at[2]

            def step_scores(b):
                sc[b, :, : s.width] = jnp.sum(logits[b] * rate, axis=0, keepdims=True)

            blocks(step_scores)
            reduce_scores = all_reduce(2, total_of)
            next(reduce_scores)
        mylanes = pl.ds(pl.multiple_of(z * s.slab, 128), s.slab)

        def fresh(k):
            each(s.z, z, lambda p: num_copy(k, p, p).wait_recv())
            first, size = parts[k]
            piece = slice(first, first + size)
            num_r[z, piece, :] = num_s[z, piece, :]
            acc = num_r[0, piece, :].astype(F32)
            for i in range(1, s.z):
                acc = acc + num_r[i, piece, :].astype(F32)
            acc = acc + PSEUDO_COUNT * held[piece, mylanes].astype(F32)
            return (acc / (mass[piece] + PSEUDO_COUNT)).astype(BF16)

        if t == 0:
            def new_copy(k, p, source, parts=parts):
                lanes = pl.ds(pl.multiple_of(source * s.slab, 128), s.slab)
                piece = cents.at[1, pl.ds(parts[k][0], parts[k][1]), lanes]
                return copy(piece, piece, ref["new_sem"], k * s.z + p, k * s.z + source, to_z(p))

            for k in range(2):
                cents[1, parts[k][0] : parts[k][0] + parts[k][1], mylanes] = fresh(k)
                each(s.z, z, lambda p: new_copy(k, p, z).start())
            for k in range(2):
                each(s.z, z, lambda p: new_copy(k, p, p).wait_recv())
        else:
            for k in range(3):
                table[core, y, x, parts[k][0] : parts[k][0] + parts[k][1], :] = fresh(k)
                if k < 2:
                    gather.start_b(k + 1)
                else:
                    gather.start_a()
        later.append((num_copy, len(parts)))
        if t == 0:
            later.append((new_copy, 2))

    next(reduce_scores)
    gather.spread(1, 1, s.y)
    gather.turn()
    gather.spread(2, 1, s.y)
    for _ in reduce_scores:
        pass
    final = ref["st_f"]
    offset = x * s.chip + core * s.rows
    n_out = 32
    here = lax.broadcasted_iota(jnp.int32, (n_out, s.span), 1)
    wanted = lax.broadcasted_iota(jnp.int32, (n_out, s.span), 0) + offset
    column = jnp.sum(jnp.where(here == wanted, final[2, y], 0.0), axis=1, keepdims=True)
    eye = lax.broadcasted_iota(jnp.int32, (n_out, 128), 0) == lax.broadcasted_iota(jnp.int32, (n_out, 128), 1)
    ref["score"][...] = jnp.sum(jnp.where(eye, column, 0.0), axis=0, keepdims=True)
    store_score = pltpu.make_async_copy(ref["score"], out_v, ref["store_sem"].at[s.z])
    store_score.start()
    gather.finish()
    picked, out_s, out_r = ref["picked"], ref["out_s"], ref["out_r"]
    out_ex = Exchange(s.z, z, to_z, ref["out_sem"], lambda p: out_s.at[p], lambda p: out_r.at[p])

    def pick(i, carry):
        p = lax.rem(z + 1 + i, s.z)
        base = (2 * p + core) * s.outs

        def eight(j, carry):
            for k in range(8):
                n = j * 8 + k
                picked[pl.ds(n, 1), :] = wide[pl.ds(pos[base + n], 1), :]
            return carry

        lax.fori_loop(0, s.outs // 8, eight, 0)
        out_s[p] = picked[...].astype(BF16)

        @pl.when(p != z)
        def _():
            copy(out_s.at[p], out_r.at[z], ref["out_sem"], p, z, to_z(p)).start()

        return carry

    lax.fori_loop(0, s.z, pick, 0)
    swap.wait_send()

    @pl.when(z // zh == core)
    def _():
        each(s.z, z, lambda p: cent_copy(z, p).wait_send())

    for exchange in pending:
        exchange.sent()
    for sent_copy, count in later:
        for k in range(count):
            each(s.z, z, lambda p: sent_copy(k, p, z).wait_send())
    def store(p, block):
        lanes = pl.ds(pl.multiple_of(p * s.slab, 128), s.slab)
        return pltpu.make_async_copy(block, out_c.at[:, lanes], ref["store_sem"].at[p])

    store(z, out_s.at[z]).start()

    def keep(i, carry):
        p = lax.rem(z + s.z - i, s.z)
        copy(out_s.at[p], out_r.at[p], ref["out_sem"], p, p, to_z(p)).wait_recv()
        store(p, out_r.at[p]).start()
        return carry

    lax.fori_loop(1, s.z, keep, 0)
    out_ex.sent()
    store_score.wait()
    store(z, out_s.at[z]).wait()
    each(s.z, z, lambda p: store(p, out_r.at[p]).wait())


def per_device(s, embeddings, outcomes, seed_index):
    core = lax.axis_index("dp") % 2
    cent = lax.axis_index("cent")
    plane = s.rows * s.x * s.y
    dp, rest = seed_index // plane, seed_index % plane
    zs, side = dp // 2, dp % 2
    zh = s.z // 2
    q = (zs // zh) * (s.x * s.y) + rest // s.rows
    r = (zs % zh) * s.chip + side * s.rows + rest % s.rows
    qr = jnp.stack([q, r])
    pos = q * s.local + r
    offset = (cent % s.x) * s.chip + core * s.rows
    spot = lax.broadcasted_iota(jnp.int32, (s.rows, s.span), 1) - lax.broadcasted_iota(
        jnp.int32, (s.rows, s.span), 0
    )
    lab = jnp.sum(
        jnp.where(spot == offset, outcomes.astype(F32)[:, None], 0.0), axis=0, keepdims=True
    )
    scratch = scratch_of(s)
    anywhere = pl.BlockSpec(memory_space=pl.ANY)
    padded = jnp.pad(embeddings, ((0, 32 - s.rows), (0, 0)))
    out_c, out_v = pl.pallas_call(
        functools.partial(kernel, s, tuple(scratch)),
        out_shape=(
            jax.ShapeDtypeStruct((s.outs, s.features), BF16),
            jax.ShapeDtypeStruct((1, 128), F32),
        ),
        in_specs=[anywhere] * 4,
        out_specs=(anywhere, anywhere),
        scratch_shapes=list(scratch.values()),
        compiler_params=pltpu.CompilerParams(
            collective_id=0, has_side_effects=True, vmem_limit_bytes=48 * 1024 * 1024
        ),
    )(padded, lab, qr, pos)
    return out_c, out_v[0, : s.rows]


def build(mesh, y, x):
    z = mesh.shape["dp"] // 2

    def run(embeddings, outcomes, seed_index):
        devices = mesh.shape["dp"] * mesh.shape["cent"]
        s = Sizes(
            z, y, x, embeddings.shape[0] // devices, embeddings.shape[1],
            seed_index.shape[0] // mesh.shape["cent"],
        )
        return jax.shard_map(
            functools.partial(per_device, s),
            mesh=mesh,
            in_specs=(P(("dp", "cent"), None), P(("dp", "cent")), P("cent")),
            out_specs=(P(("cent", "dp"), None), P(("dp", "cent"))),
            check_vma=False,
        )(embeddings, outcomes, seed_index)

    return run


def solution(mesh):
    return build(mesh, mesh.shape["cent"] // 4, 4)
```
